32 devices in a mesh: gx: 8 (over z, y), gy: 4 (over x, core).
Axes of the slice: x: 2, y: 2, z: 4, core: 2. Of those that a mesh axis runs over, the one named last changes fastest.
Arguments:
- initial_warmth_field: float32 [16, 1024, 512], P(None, 'gx', 'gy'), may hold values from -8 to 8
- horizontal_motion_pair: float32 [2, 16, 1024, 512], P(None, None, 'gx', 'gy'), may hold values from -4 to 4
- z_directed_motion: float32 [16, 1024, 512], P(None, 'gx', 'gy'), may hold values from -3 to 3
- earlier_rate_change: float32 [16, 1024, 512], P(None, 'gx', 'gy'), may hold values from -6 to 6
- layer_depth_spacing: float32 [16], replicated, may hold values from 0.5 to 2
- backward_spread_ratio: float32 [16], replicated, may hold values from 4 to 100000
- wall_warmth_bounds: float32 [2, 1024, 512], P(None, 'gx', 'gy'), may hold values from -4 to 4
Outputs:
- resulting_warmth_field: float32 [16, 1024, 512], P(None, 'gx', 'gy')
- current_rate_change: float32 [16, 1024, 512], P(None, 'gx', 'gy')
The draws below stay inside these ranges and needn't reach their ends.
All inputs are finite; a program needn't handle non-finite values.
Results may differ from the reference program's by a relative error of at most 0.000071.
Values sent between devices are 32-bit elements; how exact they have to be, the bound alone decides.
A program may use at most 64 MiB of HBM per device.

```python
import math
import jax
import jax.numpy as jnp

NZ = 16
CELLS_ALONG_X = 1024
CELLS_ALONG_Y = 512


def draw_initial_warmth_field(key, part):
    key_rough = jax.random.fold_in(key, 0)
    return jnp.clip(jax.random.normal(key_rough, (NZ, CELLS_ALONG_X, CELLS_ALONG_Y), jnp.float32), -6.0, 6.0)


def draw_backward_spread_ratio(key, part):
    exponent = jax.random.uniform(key, (NZ,), jnp.float32, math.log(4.0), math.log(100000.0))
    return jnp.clip(jnp.exp(exponent), 4.0, 100000.0)


def block_scale(key, extent, cuts, least, top_value):
    gain = 1.0
    for dim, blocks in cuts:
        heights = jax.random.uniform(jax.random.fold_in(jax.random.fold_in(key, 6), dim), (blocks,), jnp.float32, least / len(cuts), top_value / len(cuts))
        gain = gain * jnp.repeat(jnp.exp(heights), extent[dim] // blocks).reshape((-1,) + (1,) * (len(extent) - 1 - dim))
    return gain


def centred(key, extent, width, most, cuts=(), kind=jnp.bfloat16):
    result = jax.random.normal(key, extent, jnp.float32) * width
    if len(cuts) > 0:
        result = block_scale(key, extent, cuts, -0.22, 0.18) * result
    return jnp.clip(result, min=-most, max=most).astype(kind)


def setup_inputs(seed: int = 0) -> dict:
    key_list = jax.random.split(jax.random.key(seed), 8)
    return {
        "initial_warmth_field": draw_initial_warmth_field(jax.random.fold_in(key_list[7], 71), 0),
        "horizontal_motion_pair": centred(key_list[1], (2, NZ, CELLS_ALONG_X, CELLS_ALONG_Y), 1.0, 4.0, ((2, 8), (3, 4)), jnp.float32),
        "z_directed_motion": centred(key_list[2], (NZ, CELLS_ALONG_X, CELLS_ALONG_Y), 0.5, 3.0, ((1, 8), (2, 4)), jnp.float32),
        "earlier_rate_change": centred(key_list[3], (NZ, CELLS_ALONG_X, CELLS_ALONG_Y), 1.0, 6.0, ((1, 8), (2, 4)), jnp.float32),
        "layer_depth_spacing": jnp.clip(jnp.exp(jax.random.uniform(key_list[4], (NZ,), jnp.float32, math.log(0.5), math.log(2.0))), 0.5, 2.0),
        "backward_spread_ratio": draw_backward_spread_ratio(jax.random.fold_in(key_list[7], 71), 0),
        "wall_warmth_bounds": centred(key_list[6], (2, CELLS_ALONG_X, CELLS_ALONG_Y), 1.0, 4.0, ((1, 8), (2, 4)), jnp.float32),
    }


COURANT = 0.5
DIFF_Y = 0.2
DIFF_Z = 0.25
NEW_TERM_COEF = 0.75
OLD_TERM_COEF = -5.0 / 12.0


def depthwise_rate_change(initial_warmth_field, z_directed_motion, layer_depth_spacing, wall_warmth_bounds):
    inner_face_transport = (z_directed_motion[:-1] + z_directed_motion[1:]) * (initial_warmth_field[:-1] + initial_warmth_field[1:]) * 0.25
    empty_layer_sheet = jnp.zeros_like(initial_warmth_field[:1])
    flux_up = jnp.concatenate([empty_layer_sheet, inner_face_transport, empty_layer_sheet], 0)
    spacing = layer_depth_spacing[:, None, None]
    carry_through_depth = (flux_up[1:] - flux_up[:-1]) / spacing
    warmth_with_ghosts = jnp.concatenate([wall_warmth_bounds[:1], initial_warmth_field, wall_warmth_bounds[1:]], 0)
    midway_average = jnp.concatenate([layer_depth_spacing[:1], 0.5 * (layer_depth_spacing[:-1] + layer_depth_spacing[1:]), layer_depth_spacing[-1:]], 0)
    gradient_at_faces = (warmth_with_ghosts[1:] - warmth_with_ghosts[:-1]) / midway_average[:, None, None]
    thermal_spreading_step = (gradient_at_faces[1:] - gradient_at_faces[:-1]) / spacing
    return carry_through_depth, thermal_spreading_step


def reference(initial_warmth_field, horizontal_motion_pair, z_directed_motion, earlier_rate_change, layer_depth_spacing, backward_spread_ratio, wall_warmth_bounds):
    x_directed_motion = horizontal_motion_pair[0]
    y_directed_motion = horizontal_motion_pair[1]
    x_directed_transport = (x_directed_motion + jnp.roll(x_directed_motion, -1, 1)) * (initial_warmth_field + jnp.roll(initial_warmth_field, -1, 1)) * 0.25
    y_directed_transport = (y_directed_motion + jnp.roll(y_directed_motion, -1, 2)) * (initial_warmth_field + jnp.roll(initial_warmth_field, -1, 2)) * 0.25
    advect_xy = (x_directed_transport - jnp.roll(x_directed_transport, 1, 1)) + (y_directed_transport - jnp.roll(y_directed_transport, 1, 2))
    carry_through_depth, thermal_spreading_step = depthwise_rate_change(initial_warmth_field, z_directed_motion, layer_depth_spacing, wall_warmth_bounds)
    stacked_layer_count = jnp.roll(initial_warmth_field, -1, 2) - 2.0 * initial_warmth_field + jnp.roll(initial_warmth_field, 1, 2)
    current_rate_change = -COURANT * (advect_xy + carry_through_depth) + DIFF_Y * stacked_layer_count + DIFF_Z * thermal_spreading_step
    linear_system_source = initial_warmth_field + NEW_TERM_COEF * current_rate_change + OLD_TERM_COEF * earlier_rate_change
    cyclic_row_extent = linear_system_source.shape[1]
    spectral_coefficients = jnp.fft.rfft(linear_system_source, axis=1)
    angle_step = jnp.arange(cyclic_row_extent // 2 + 1, dtype=jnp.float32) * (math.pi / cyclic_row_extent)
    spectral_symbol = 1.0 + 4.0 * backward_spread_ratio[:, None, None] * (jnp.sin(angle_step) ** 2)[None, :, None]
    resulting_warmth_field = jnp.fft.irfft(spectral_coefficients / spectral_symbol, n=cyclic_row_extent, axis=1).astype(jnp.float32)
    return resulting_warmth_field, current_rate_change
```

```python
import functools

import jax
import jax.numpy as jnp
from jax import lax
from jax.experimental import pallas as pl
from jax.experimental.pallas import tpu as pltpu
from jax.sharding import PartitionSpec as P

COURANT = 0.5
DIFF_Y = 0.2
DIFF_Z = 0.25
NEW_TERM_COEF = 0.75
OLD_TERM_COEF = -5.0 / 12.0

MESH = pl.DeviceIdType.MESH
F32 = jnp.float32
BF16 = jnp.bfloat16
GROUPS = 4


def lanes_of(shape):
    return lax.broadcasted_iota(jnp.int32, shape, len(shape) - 1)


def rows_of(shape):
    return lax.broadcasted_iota(jnp.int32, shape, len(shape) - 2)


def kernel(
    nx, ny, nz, m,
    t_hbm, uv_hbm, w_hbm, old_hbm, dz_ref, r_ref, wall_hbm,
    x_hbm, c_hbm,
    t, uv, w, old, cur, rhs, f_tab, g_tab, green, theta, scale, inv_dz, inv_between,
    pack, pack_got, edge, edge_got, edge_fix, side_fix, moment, moment_got, far,
    in_sem, out_sem, halo_send, halo_recv, moment_send, moment_recv,
):
    gx = lax.axis_index("gx")
    gy = lax.axis_index("gy")
    east, west = lax.rem(gx + 1, nx), lax.rem(gx + nx - 1, nx)
    north, south = lax.rem(gy + 1, ny), lax.rem(gy + ny - 1, ny)
    q_rows = m // 4

    loads = [
        pltpu.make_async_copy(t_hbm, t.at[pl.ds(1, nz)], in_sem.at[0]),
        pltpu.make_async_copy(uv_hbm, uv, in_sem.at[1]),
        pltpu.make_async_copy(wall_hbm.at[pl.ds(0, 1)], t.at[pl.ds(0, 1)], in_sem.at[2]),
        pltpu.make_async_copy(wall_hbm.at[pl.ds(1, 1)], t.at[pl.ds(nz + 1, 1)], in_sem.at[3]),
        pltpu.make_async_copy(w_hbm, w.at[pl.ds(1, nz)], in_sem.at[4]),
        pltpu.make_async_copy(old_hbm, old, in_sem.at[5]),
    ]
    for load in loads:
        load.start()

    barrier = pltpu.get_barrier_semaphore()
    for s in range(1, nx):
        pl.semaphore_signal(
            barrier, inc=1, device_id={"gx": lax.rem(gx + s, nx)}, device_id_type=MESH
        )
    for j in (north, south):
        pl.semaphore_signal(barrier, inc=1, device_id={"gy": j}, device_id_type=MESH)

    for k in range(nz):
        scale[k:k + 1, :] = jnp.full((1, m), r_ref[k], F32)
        inv_dz[k:k + 1, :] = 1.0 / jnp.full((1, m), dz_ref[k], F32)
    inv_between[0:1, :] = inv_dz[0:1, :]
    inv_between[nz:nz + 1, :] = inv_dz[nz - 1:nz, :]
    for k in range(nz - 1):
        inv_between[k + 1:k + 2, :] = 2.0 / jnp.full((1, m), dz_ref[k] + dz_ref[k + 1], F32)
    r = scale[...]
    s = 0.5 / jnp.sqrt(r)
    theta[...] = 2.0 * jnp.log1p(s + s * s / (1.0 + jnp.sqrt(1.0 + s * s)))
    scale[...] = 1.0 / jnp.sqrt(1.0 + 4.0 * r)

    def make_tables(k, carry):
        th = theta[pl.ds(k, 1), :]
        row = rows_of((m, m))
        lane = lanes_of((m, m))
        f_tab[k] = jnp.exp(-th * row.astype(F32))
        g_tab[k] = jnp.exp(-th * (m - 1 - row).astype(F32))
        full = scale[pl.ds(k, 1), :] * jnp.exp(-th * jnp.abs(row - lane).astype(F32))
        high = full.astype(BF16)
        green[k, :, 0:m] = high
        green[k, :, m:2 * m] = (full - high.astype(F32)).astype(BF16)
        return carry

    lax.fori_loop(0, nz, make_tables, 0)

    loads[0].wait()
    loads[1].wait()

    def make_pack(k, carry):
        pt, pv = carry
        pair = lanes_of((q_rows, m)) // 2
        for h in range(4):
            rows = slice(h * q_rows, (h + 1) * q_rows)
            turn = 32 * h + 2 * k + 1
            mine = pair == 16 * h + k
            pt = jnp.where(mine, pltpu.roll(t[k + 1, rows, :], turn, 1), pt)
            pv = jnp.where(mine, pltpu.roll(uv[1, k, rows, :], turn, 1), pv)
        edge[0, 0, pl.ds(k, 1), :] = t[k + 1, m - 1:m, :]
        edge[0, 1, pl.ds(k, 1), :] = uv[0, k, m - 1:m, :]
        edge[1, 0, pl.ds(k, 1), :] = t[k + 1, 0:1, :]
        edge[1, 1, pl.ds(k, 1), :] = uv[0, k, 0:1, :]
        return pt, pv

    blank = jnp.zeros((q_rows, m), F32)
    pt, pv = lax.fori_loop(0, nz, make_pack, (blank, blank))
    pack[0] = pt
    pack[1] = pv

    pl.semaphore_wait(barrier, nx + 1)

    def halo(src, dst, i, where):
        copy = pltpu.make_async_remote_copy(
            src_ref=src, dst_ref=dst, send_sem=halo_send.at[i], recv_sem=halo_recv.at[i],
            device_id=where, device_id_type=MESH,
        )
        copy.start()
        return copy

    halos = [
        halo(pack, pack_got.at[0], 0, {"gy": north}),
        halo(pack, pack_got.at[1], 1, {"gy": south}),
        halo(edge.at[0], edge_got.at[0], 2, {"gx": east}),
        halo(edge.at[1], edge_got.at[1], 3, {"gx": west}),
    ]

    for load in loads[2:]:
        load.wait()
    w[0] = -w[1]
    w[nz + 1] = -w[nz]

    def inner(k, carry):
        row = rows_of((m, m))
        lane = lanes_of((m, m))
        here = t[k + 1]
        u = uv[0, k]
        v = uv[1, k]
        fx = (u + pltpu.roll(u, m - 1, 0)) * (here + pltpu.roll(here, m - 1, 0))
        fx = jnp.where(row == m - 1, 0.0, fx)
        right = pltpu.roll(here, m - 1, 1)
        fy = (v + pltpu.roll(v, m - 1, 1)) * (here + right)
        fy = jnp.where(lane == m - 1, 0.0, fy)
        div = (fx - pltpu.roll(fx, 1, 0)) + (fy - pltpu.roll(fy, 1, 1))
        lap = (
            jnp.where(lane == m - 1, 0.0, right)
            + jnp.where(lane == 0, 0.0, pltpu.roll(here, 1, 1))
            - 2.0 * here
        )
        below, above = t[k], t[k + 2]
        wk = w[k + 1]
        fz = (wk + w[k + 2]) * (here + above) - (w[k] + wk) * (below + here)
        slope = (above - here) * inv_between[pl.ds(k + 1, 1), :] - (here - below) * inv_between[
            pl.ds(k, 1), :
        ]
        idz = inv_dz[pl.ds(k, 1), :]
        value = (
            (-0.25 * COURANT) * (div + fz * idz) + DIFF_Y * lap + DIFF_Z * (slope * idz)
        )
        b = here + NEW_TERM_COEF * value + OLD_TERM_COEF * old[k]
        cur[k] = value
        rhs[k] = b
        moment[0, pl.ds(k, 1), :] = jnp.sum(g_tab[k] * b, axis=0, keepdims=True)
        moment[1, pl.ds(k, 1), :] = jnp.sum(f_tab[k] * b, axis=0, keepdims=True)
        return carry

    lax.fori_loop(0, nz, inner, 0)

    lane1 = lanes_of((1, m))
    th_lane = jnp.zeros((1, m), F32)
    for k in range(nz):
        th_lane = jnp.where(lax.rem(lane1, 32) // 2 == k, theta[k:k + 1, :], th_lane)
    cell = rows_of((q_rows, m)) + (lanes_of((q_rows, m)) // 32) * q_rows
    weight_f = NEW_TERM_COEF * jnp.exp(-th_lane * cell.astype(F32))
    weight_g = NEW_TERM_COEF * jnp.exp(-th_lane * (m - 1 - cell).astype(F32))
    th = theta[...]
    q_end = jnp.exp(-(m - 1.0) * th)

    for copy in halos:
        copy.wait_recv()

    first = lax.rem(lanes_of((q_rows, m)), 2) == 1
    near_t = jnp.where(
        first, pltpu.roll(pack_got[0, 0], 1, 1), pltpu.roll(pack_got[1, 0], m - 1, 1)
    )
    near_v = jnp.where(
        first, pltpu.roll(pack_got[0, 1], 1, 1), pltpu.roll(pack_got[1, 1], m - 1, 1)
    )
    flux = (pack[1] + near_v) * (pack[0] + near_t)
    fix = DIFF_Y * near_t + jnp.where(first, 0.25 * COURANT, -0.25 * COURANT) * flux
    side_fix[...] = fix
    low = (0.25 * COURANT) * (edge_got[0, 1] + edge[1, 1]) * (edge_got[0, 0] + edge[1, 0])
    top = (-0.25 * COURANT) * (edge_got[1, 1] + edge[0, 1]) * (edge_got[1, 0] + edge[0, 0])
    edge_fix[0] = low
    edge_fix[1] = top

    level = rows_of((nz, m))
    lane = lanes_of((nz, m))

    def spread(weights):
        line = jnp.sum(weights * fix, axis=0, keepdims=True)
        line = line + pltpu.roll(line, 32, 1)
        line = line + pltpu.roll(line, 64, 1)
        wide = jnp.broadcast_to(line, (nz, m))
        last = jnp.sum(jnp.where(lane == 2 * level, wide, 0.0), axis=1, keepdims=True)
        head = jnp.sum(jnp.where(lane == 2 * level + 1, wide, 0.0), axis=1, keepdims=True)
        return jnp.where(lane == 0, head, 0.0) + jnp.where(lane == m - 1, last, 0.0)

    moment[0] = moment[0] + NEW_TERM_COEF * (q_end * low + top) + spread(weight_g)
    moment[1] = moment[1] + NEW_TERM_COEF * (low + q_end * top) + spread(weight_f)

    sends = []
    for s in range(1, nx):
        copy = pltpu.make_async_remote_copy(
            src_ref=moment, dst_ref=moment_got.at[s - 1],
            send_sem=moment_send.at[s - 1], recv_sem=moment_recv.at[s - 1],
            device_id={"gx": lax.rem(gx + s, nx)}, device_id_type=MESH,
        )
        copy.start()
        sends.append(copy)

    def local_solve(k, carry):
        lane = lanes_of((q_rows, m))
        row = rows_of((q_rows, m))
        side = (lane == 0) | (lane == m - 1)
        parts = []
        for h in range(4):
            rows = slice(h * q_rows, (h + 1) * q_rows)
            extra = jnp.where(
                side, pltpu.roll(side_fix[...], m - 1 - 32 * h - 2 * k, 1), 0.0
            )
            if h == 0:
                extra = extra + jnp.where(row == 0, edge_fix[0, pl.ds(k, 1), :], 0.0)
            if h == 3:
                extra = extra + jnp.where(row == q_rows - 1, edge_fix[1, pl.ds(k, 1), :], 0.0)
            cur[k, rows, :] = cur[k, rows, :] + extra
            parts.append(rhs[k, rows, :] + NEW_TERM_COEF * extra)
        b = jnp.concatenate(parts, axis=0)
        high = b.astype(BF16)
        pair = jnp.concatenate([high, (b - high.astype(F32)).astype(BF16)], axis=1)
        both = jnp.dot(
            green[k], jnp.concatenate([pair, pair], axis=0), preferred_element_type=F32
        )
        rhs[k] = both[:, 0:m] + both[:, m:2 * m]
        return carry

    per = nz // GROUPS
    stores = []
    for part in range(GROUPS):
        lax.fori_loop(part * per, (part + 1) * per, local_solve, 0)
        span = pl.ds(part * per, per)
        store = pltpu.make_async_copy(cur.at[span], c_hbm.at[span], out_sem.at[part])
        store.start()
        stores.append(store)

    step = jnp.exp(-float(m) * th)
    share = scale[...] * jnp.exp(-th) / (1.0 - jnp.exp(-float(m * nx) * th))
    powers = [jnp.ones_like(step)]
    for s in range(1, nx):
        powers.append(powers[-1] * step)
    from_low = powers[nx - 1] * moment[0]
    from_high = powers[nx - 1] * moment[1]

    for copy in sends:
        copy.wait_recv()
    for s in range(1, nx):
        from_low = from_low + powers[s - 1] * moment_got[s - 1, 0]
        from_high = from_high + powers[nx - s - 1] * moment_got[s - 1, 1]
    far[0] = share * from_low
    far[1] = share * from_high

    def finish(k, carry):
        rhs[k] = (
            rhs[k]
            + f_tab[k] * far[0, pl.ds(k, 1), :]
            + g_tab[k] * far[1, pl.ds(k, 1), :]
        )
        return carry

    for part in range(GROUPS):
        lax.fori_loop(part * per, (part + 1) * per, finish, 0)
        span = pl.ds(part * per, per)
        store = pltpu.make_async_copy(rhs.at[span], x_hbm.at[span], out_sem.at[GROUPS + part])
        store.start()
        stores.append(store)

    for copy in halos + sends:
        copy.wait_send()
    for store in stores:
        store.wait()


def on_device(
    initial_warmth_field,
    horizontal_motion_pair,
    z_directed_motion,
    earlier_rate_change,
    layer_depth_spacing,
    backward_spread_ratio,
    wall_warmth_bounds,
):
    nx = lax.axis_size("gx")
    ny = lax.axis_size("gy")
    nz, m, width = initial_warmth_field.shape
    assert nz == 16 and m == 128 and width == 128
    block = jax.ShapeDtypeStruct((nz, m, m), F32)
    anywhere = pl.BlockSpec(memory_space=pl.ANY)
    scalars = pl.BlockSpec(memory_space=pltpu.SMEM)
    field = pltpu.VMEM((nz, m, m), F32)
    return pl.pallas_call(
        functools.partial(kernel, nx, ny, nz, m),
        out_shape=(block, block),
        in_specs=[anywhere] * 4 + [scalars] * 2 + [anywhere],
        out_specs=(anywhere, anywhere),
        scratch_shapes=[
            pltpu.VMEM((nz + 2, m, m), F32),
            pltpu.VMEM((2, nz, m, m), F32),
            pltpu.VMEM((nz + 2, m, m), F32),
            field, field, field, field, field,
            pltpu.VMEM((nz, m, 2 * m), BF16),
            pltpu.VMEM((nz, m), F32),
            pltpu.VMEM((nz, m), F32),
            pltpu.VMEM((nz, m), F32),
            pltpu.VMEM((nz + 8, m), F32),
            pltpu.VMEM((2, m // 4, m), F32),
            pltpu.VMEM((2, 2, m // 4, m), F32),
            pltpu.VMEM((2, 2, nz, m), F32),
            pltpu.VMEM((2, 2, nz, m), F32),
            pltpu.VMEM((2, nz, m), F32),
            pltpu.VMEM((m // 4, m), F32),
            pltpu.VMEM((2, nz, m), F32),
            pltpu.VMEM((nx - 1, 2, nz, m), F32),
            pltpu.VMEM((2, nz, m), F32),
            pltpu.SemaphoreType.DMA((6,)),
            pltpu.SemaphoreType.DMA((2 * GROUPS,)),
            pltpu.SemaphoreType.DMA((4,)),
            pltpu.SemaphoreType.DMA((4,)),
            pltpu.SemaphoreType.DMA((nx - 1,)),
            pltpu.SemaphoreType.DMA((nx - 1,)),
        ],
        compiler_params=pltpu.CompilerParams(
            collective_id=0, has_side_effects=True, vmem_limit_bytes=40 * 1024 * 1024
        ),
        cost_estimate=pl.CostEstimate(
            flops=16 * 2 * 128 * 256 * 256, bytes_accessed=8 * 1024 * 1024, transcendentals=0
        ),
    )(
        initial_warmth_field,
        horizontal_motion_pair,
        z_directed_motion,
        earlier_rate_change,
        layer_depth_spacing,
        backward_spread_ratio,
        wall_warmth_bounds,
    )


def solution(mesh):
    in_specs = (
        P(None, "gx", "gy"),
        P(None, None, "gx", "gy"),
        P(None, "gx", "gy"),
        P(None, "gx", "gy"),
        P(),
        P(),
        P(None, "gx", "gy"),
    )
    out_specs = (P(None, "gx", "gy"), P(None, "gx", "gy"))
    return jax.shard_map(
        on_device, mesh=mesh, in_specs=in_specs, out_specs=out_specs, check_vma=False
    )
```

```python
import functools

import jax
import jax.numpy as jnp
from jax import lax
from jax.experimental import pallas as pl
from jax.experimental.pallas import tpu as pltpu
from jax.sharding import PartitionSpec as P

COURANT = 0.5
DIFF_Y = 0.2
DIFF_Z = 0.25
NEW_TERM_COEF = 0.75
OLD_TERM_COEF = -5.0 / 12.0

MESH = pl.DeviceIdType.MESH
F32 = jnp.float32
BF16 = jnp.bfloat16
GROUPS = 4
OFF = 8


def lanes_of(shape):
    return lax.broadcasted_iota(jnp.int32, shape, len(shape) - 1)


def rows_of(shape):
    return lax.broadcasted_iota(jnp.int32, shape, len(shape) - 2)


def kernel(
    nx, ny, nz, m,
    t_hbm, uv_hbm, w_hbm, old_hbm, dz_hbm, r_hbm, wall_hbm,
    x_hbm, c_hbm,
    t, u_all, v_all, w, old, cur, rhs, green, head_pow, tail_pow, block_pow, far_block,
    theta, scale, inv_dz, up_coef, down_coef,
    pack, pack_got, edge, edge_got, edge_fix, side_fix, moment, moment_got,
    dz_ref, r_ref,
    in_sem, out_sem, halo_send, halo_recv, moment_send, moment_recv,
):
    gx = lax.axis_index("gx")
    gy = lax.axis_index("gy")
    east, west = lax.rem(gx + 1, nx), lax.rem(gx + nx - 1, nx)
    north, south = lax.rem(gy + 1, ny), lax.rem(gy + ny - 1, ny)
    q_rows = m // 4
    blocks = m // 8
    inside = pl.ds(OFF, m)

    loads = [
        pltpu.make_async_copy(r_hbm, r_ref, in_sem.at[0]),
        pltpu.make_async_copy(dz_hbm, dz_ref, in_sem.at[1]),
        pltpu.make_async_copy(t_hbm, t.at[pl.ds(1, nz), inside], in_sem.at[2]),
        pltpu.make_async_copy(uv_hbm.at[1], v_all, in_sem.at[3]),
        pltpu.make_async_copy(uv_hbm.at[0], u_all.at[:, inside], in_sem.at[4]),
        pltpu.make_async_copy(wall_hbm.at[0], t.at[0, inside], in_sem.at[5]),
        pltpu.make_async_copy(wall_hbm.at[1], t.at[nz + 1, inside], in_sem.at[6]),
        pltpu.make_async_copy(w_hbm, w.at[pl.ds(1, nz)], in_sem.at[7]),
        pltpu.make_async_copy(old_hbm, old, in_sem.at[8]),
    ]
    for load in loads:
        load.start()

    barrier = pltpu.get_barrier_semaphore()
    for s in range(1, nx):
        pl.semaphore_signal(
            barrier, inc=1, device_id={"gx": lax.rem(gx + s, nx)}, device_id_type=MESH
        )
    for j in (north, south):
        pl.semaphore_signal(barrier, inc=1, device_id={"gy": j}, device_id_type=MESH)

    loads[0].wait()
    loads[1].wait()
    for k in range(nz):
        scale[k:k + 1, :] = jnp.full((1, m), r_ref[k], F32)
        inv_dz[k:k + 1, :] = 1.0 / jnp.full((1, m), dz_ref[k], F32)
    down_coef[0:1, :] = inv_dz[0:1, :]
    up_coef[nz - 1:nz, :] = inv_dz[nz - 1:nz, :]
    for k in range(nz - 1):
        between = 2.0 / jnp.full((1, m), dz_ref[k] + dz_ref[k + 1], F32)
        up_coef[k:k + 1, :] = between
        down_coef[k + 1:k + 2, :] = between
    up_coef[...] = DIFF_Z * up_coef[...] * inv_dz[...]
    down_coef[...] = DIFF_Z * down_coef[...] * inv_dz[...]
    inv_dz[...] = (-0.25 * COURANT) * inv_dz[...]
    r = scale[...]
    s = 0.5 / jnp.sqrt(r)
    theta[...] = 2.0 * jnp.log1p(s + s * s / (1.0 + jnp.sqrt(1.0 + s * s)))
    scale[...] = 1.0 / jnp.sqrt(1.0 + 4.0 * r)
    th = theta[...]
    for b in range(blocks):
        block_pow[b] = jnp.exp((-8.0 * b) * th)

    def make_tables(k, carry):
        row = rows_of((8, m))
        lane = lanes_of((8, m))
        th = theta[pl.ds(k, 1), :]
        head_pow[k] = jnp.exp(-th * row.astype(F32))
        tail_pow[k] = jnp.exp(-th * (7 - row).astype(F32))
        level_scale = scale[pl.ds(k, 1), :]
        near = level_scale * jnp.exp(-th * jnp.abs(row - lane).astype(F32))
        wrap = level_scale * jnp.exp(-th * (row - lane + m).astype(F32))
        for b in range(0, blocks, 2):
            full = jnp.concatenate(
                [
                    pltpu.roll(jnp.where(lane < m - 8 * c, near, wrap), 8 * c, 1)
                    if c
                    else near
                    for c in (b, b + 1)
                ],
                axis=0,
            )
            high = full.astype(BF16)
            green[k, 8 * b:8 * b + 16, 0:m] = high
            green[k, 8 * b:8 * b + 16, m:2 * m] = (full - high.astype(F32)).astype(BF16)
        return carry

    lax.fori_loop(0, nz, make_tables, 0)

    for load in loads[2:5]:
        load.wait()

    def make_pack(k, carry):
        pt, pv = carry
        pair = lanes_of((q_rows, m)) // 2
        for h in range(4):
            turn = 32 * h + 2 * k + 1
            mine = pair == 16 * h + k
            here = t[k + 1, OFF + h * q_rows:OFF + (h + 1) * q_rows, :]
            pt = jnp.where(mine, pltpu.roll(here, turn, 1), pt)
            pv = jnp.where(
                mine, pltpu.roll(v_all[k, h * q_rows:(h + 1) * q_rows, :], turn, 1), pv
            )
        edge[0, 0, pl.ds(k, 1), :] = t[k + 1, OFF + m - 1:OFF + m, :]
        edge[0, 1, pl.ds(k, 1), :] = u_all[k, OFF + m - 1:OFF + m, :]
        edge[1, 0, pl.ds(k, 1), :] = t[k + 1, OFF:OFF + 1, :]
        edge[1, 1, pl.ds(k, 1), :] = u_all[k, OFF:OFF + 1, :]
        return pt, pv

    blank = jnp.zeros((q_rows, m), F32)
    pt, pv = lax.fori_loop(0, nz, make_pack, (blank, blank))
    pack[0] = pt
    pack[1] = pv

    pl.semaphore_wait(barrier, nx + 1)

    def halo(src, dst, i, where):
        copy = pltpu.make_async_remote_copy(
            src_ref=src, dst_ref=dst, send_sem=halo_send.at[i], recv_sem=halo_recv.at[i],
            device_id=where, device_id_type=MESH,
        )
        copy.start()
        return copy

    halos = [
        halo(pack, pack_got.at[0], 0, {"gy": north}),
        halo(pack, pack_got.at[1], 1, {"gy": south}),
        halo(edge.at[0], edge_got.at[0], 2, {"gx": east}),
        halo(edge.at[1], edge_got.at[1], 3, {"gx": west}),
    ]

    for load in loads[5:]:
        load.wait()
    w[0] = -w[1]
    w[nz + 1] = -w[nz]

    def inner(k, carry):
        row = rows_of((q_rows, m))
        lane = lanes_of((q_rows, m))
        one = pl.ds(k, 1)
        up, down, idz = up_coef[one, :], down_coef[one, :], inv_dz[one, :]
        low_sum = jnp.zeros((8, m), F32)
        high_sum = jnp.zeros((8, m), F32)
        for h in range(4):
            rows = slice(h * q_rows, (h + 1) * q_rows)
            pad = slice(OFF + h * q_rows, OFF + (h + 1) * q_rows)
            after = slice(OFF + h * q_rows + 1, OFF + (h + 1) * q_rows + 1)
            before = slice(OFF + h * q_rows - 1, OFF + (h + 1) * q_rows - 1)
            here = t[k + 1, pad, :]
            u = u_all[k, pad, :]
            v = v_all[k, rows, :]
            fx = (u + u_all[k, after, :]) * (here + t[k + 1, after, :])
            gx_flux = (u_all[k, before, :] + u) * (t[k + 1, before, :] + here)
            if h == 3:
                fx = jnp.where(row == q_rows - 1, 0.0, fx)
            if h == 0:
                gx_flux = jnp.where(row == 0, 0.0, gx_flux)
            right = pltpu.roll(here, m - 1, 1)
            fy = (v + pltpu.roll(v, m - 1, 1)) * (here + right)
            fy = jnp.where(lane == m - 1, 0.0, fy)
            div = (fx - gx_flux) + (fy - pltpu.roll(fy, 1, 1))
            lap = jnp.where(lane == m - 1, 0.0, right) + jnp.where(
                lane == 0, 0.0, pltpu.roll(here, 1, 1)
            )
            below, above = t[k, pad, :], t[k + 2, pad, :]
            wk = w[k + 1, rows, :]
            fz = (wk + w[k + 2, rows, :]) * (here + above) - (w[k, rows, :] + wk) * (below + here)
            value = (
                (-0.25 * COURANT) * div
                + idz * fz
                + DIFF_Y * (lap - 2.0 * here)
                + (up * (above - here) - down * (here - below))
            )
            b = here + NEW_TERM_COEF * value + OLD_TERM_COEF * old[k, rows, :]
            cur[k, rows, :] = value
            rhs[k, rows, :] = b
            for i in range(4):
                c = 4 * h + i
                part = b[8 * i:8 * i + 8, :]
                low_sum = low_sum + block_pow[blocks - 1 - c, one, :] * part
                high_sum = high_sum + block_pow[c, one, :] * part
        moment[0, one, :] = jnp.sum(tail_pow[k] * low_sum, axis=0, keepdims=True)
        moment[1, one, :] = jnp.sum(head_pow[k] * high_sum, axis=0, keepdims=True)
        return carry

    lax.fori_loop(0, nz, inner, 0)

    lane1 = lanes_of((1, m))
    th_lane = jnp.zeros((1, m), F32)
    for k in range(nz):
        th_lane = jnp.where(lax.rem(lane1, 32) // 2 == k, theta[k:k + 1, :], th_lane)
    cell = rows_of((q_rows, m)) + (lanes_of((q_rows, m)) // 32) * q_rows
    weight_f = NEW_TERM_COEF * jnp.exp(-th_lane * cell.astype(F32))
    weight_g = NEW_TERM_COEF * jnp.exp(-th_lane * (m - 1 - cell).astype(F32))
    q_end = jnp.exp(-(m - 1.0) * th)

    for copy in halos:
        copy.wait_recv()

    first = lax.rem(lanes_of((q_rows, m)), 2) == 1
    near_t = jnp.where(
        first, pltpu.roll(pack_got[0, 0], 1, 1), pltpu.roll(pack_got[1, 0], m - 1, 1)
    )
    near_v = jnp.where(
        first, pltpu.roll(pack_got[0, 1], 1, 1), pltpu.roll(pack_got[1, 1], m - 1, 1)
    )
    flux = (pack[1] + near_v) * (pack[0] + near_t)
    fix = DIFF_Y * near_t + jnp.where(first, 0.25 * COURANT, -0.25 * COURANT) * flux
    side_fix[...] = fix
    low = (0.25 * COURANT) * (edge_got[0, 1] + edge[1, 1]) * (edge_got[0, 0] + edge[1, 0])
    top = (-0.25 * COURANT) * (edge_got[1, 1] + edge[0, 1]) * (edge_got[1, 0] + edge[0, 0])
    edge_fix[0] = low
    edge_fix[1] = top

    level = rows_of((nz, m))
    lane = lanes_of((nz, m))

    def spread(weights):
        line = jnp.sum(weights * fix, axis=0, keepdims=True)
        line = line + pltpu.roll(line, 32, 1)
        line = line + pltpu.roll(line, 64, 1)
        wide = jnp.broadcast_to(line, (nz, m))
        last = jnp.sum(jnp.where(lane == 2 * level, wide, 0.0), axis=1, keepdims=True)
        head = jnp.sum(jnp.where(lane == 2 * level + 1, wide, 0.0), axis=1, keepdims=True)
        return jnp.where(lane == 0, head, 0.0) + jnp.where(lane == m - 1, last, 0.0)

    moment[0] = moment[0] + NEW_TERM_COEF * (q_end * low + top) + spread(weight_g)
    moment[1] = moment[1] + NEW_TERM_COEF * (low + q_end * top) + spread(weight_f)

    sends = []
    for s in range(1, nx):
        copy = pltpu.make_async_remote_copy(
            src_ref=moment, dst_ref=moment_got.at[s - 1],
            send_sem=moment_send.at[s - 1], recv_sem=moment_recv.at[s - 1],
            device_id={"gx": lax.rem(gx + s, nx)}, device_id_type=MESH,
        )
        copy.start()
        sends.append(copy)

    def local_solve(k, carry):
        lane = lanes_of((q_rows, m))
        row = rows_of((q_rows, m))
        side = (lane == 0) | (lane == m - 1)
        parts = []
        for h in range(4):
            rows = slice(h * q_rows, (h + 1) * q_rows)
            extra = jnp.where(
                side, pltpu.roll(side_fix[...], m - 1 - 32 * h - 2 * k, 1), 0.0
            )
            if h == 0:
                extra = extra + jnp.where(row == 0, edge_fix[0, pl.ds(k, 1), :], 0.0)
            if h == 3:
                extra = extra + jnp.where(row == q_rows - 1, edge_fix[1, pl.ds(k, 1), :], 0.0)
            cur[k, rows, :] = cur[k, rows, :] + extra
            parts.append(rhs[k, rows, :] + NEW_TERM_COEF * extra)
        b = jnp.concatenate(parts, axis=0)
        high = b.astype(BF16)
        pair = jnp.concatenate([high, (b - high.astype(F32)).astype(BF16)], axis=1)
        both = jnp.dot(
            green[k], jnp.concatenate([pair, pair], axis=0), preferred_element_type=F32
        )
        rhs[k] = both[:, 0:m] + both[:, m:2 * m]
        return carry

    per = nz // GROUPS
    stores = []
    for part in range(GROUPS):
        lax.fori_loop(part * per, (part + 1) * per, local_solve, 0)
        span = pl.ds(part * per, per)
        store = pltpu.make_async_copy(cur.at[span], c_hbm.at[span], out_sem.at[part])
        store.start()
        stores.append(store)

    step = jnp.exp(-float(m) * th)
    share = scale[...] * jnp.exp(-th) / (1.0 - jnp.exp(-float(m * nx) * th))
    powers = [jnp.ones_like(step)]
    for s in range(1, nx):
        powers.append(powers[-1] * step)
    from_low = powers[nx - 1] * moment[0]
    from_high = powers[nx - 1] * moment[1]

    for copy in sends:
        copy.wait_recv()
    for s in range(1, nx):
        from_low = from_low + powers[s - 1] * moment_got[s - 1, 0]
        from_high = from_high + powers[nx - s - 1] * moment_got[s - 1, 1]
    from_low = share * from_low
    from_high = share * from_high
    for b in range(blocks):
        far_block[0, b] = block_pow[b] * from_low
        far_block[1, b] = block_pow[blocks - 1 - b] * from_high

    def finish(k, carry):
        head = head_pow[k]
        tail = tail_pow[k]
        for b in range(blocks):
            rows = slice(8 * b, 8 * b + 8)
            rhs[k, rows, :] = (
                rhs[k, rows, :]
                + head * far_block[0, b, pl.ds(k, 1), :]
                + tail * far_block[1, b, pl.ds(k, 1), :]
            )
        return carry

    for part in range(GROUPS):
        lax.fori_loop(part * per, (part + 1) * per, finish, 0)
        span = pl.ds(part * per, per)
        store = pltpu.make_async_copy(rhs.at[span], x_hbm.at[span], out_sem.at[GROUPS + part])
        store.start()
        stores.append(store)

    for copy in halos + sends:
        copy.wait_send()
    for store in stores:
        store.wait()


def on_device(
    initial_warmth_field,
    horizontal_motion_pair,
    z_directed_motion,
    earlier_rate_change,
    layer_depth_spacing,
    backward_spread_ratio,
    wall_warmth_bounds,
):
    nx = lax.axis_size("gx")
    ny = lax.axis_size("gy")
    nz, m, width = initial_warmth_field.shape
    assert nz == 16 and m == 128 and width == 128
    block = jax.ShapeDtypeStruct((nz, m, m), F32)
    anywhere = pl.BlockSpec(memory_space=pl.ANY)
    far_away = pl.BlockSpec(memory_space=pltpu.HBM)
    field = pltpu.VMEM((nz, m, m), F32)
    row = pltpu.VMEM((nz, m), F32)
    return pl.pallas_call(
        functools.partial(kernel, nx, ny, nz, m),
        out_shape=(block, block),
        in_specs=[far_away] * 7,
        out_specs=(anywhere, anywhere),
        scratch_shapes=[
            pltpu.VMEM((nz + 2, m + 2 * OFF, m), F32),
            pltpu.VMEM((nz, m + 2 * OFF, m), F32),
            field,
            pltpu.VMEM((nz + 2, m, m), F32),
            field, field, field,
            pltpu.VMEM((nz, m, 2 * m), BF16),
            pltpu.VMEM((nz, 8, m), F32),
            pltpu.VMEM((nz, 8, m), F32),
            pltpu.VMEM((m // 8, nz, m), F32),
            pltpu.VMEM((2, m // 8, nz, m), F32),
            row, row, row, row, row,
            pltpu.VMEM((2, m // 4, m), F32),
            pltpu.VMEM((2, 2, m // 4, m), F32),
            pltpu.VMEM((2, 2, nz, m), F32),
            pltpu.VMEM((2, 2, nz, m), F32),
            pltpu.VMEM((2, nz, m), F32),
            pltpu.VMEM((m // 4, m), F32),
            pltpu.VMEM((2, nz, m), F32),
            pltpu.VMEM((nx - 1, 2, nz, m), F32),
            pltpu.SMEM((nz,), F32),
            pltpu.SMEM((nz,), F32),
            pltpu.SemaphoreType.DMA((9,)),
            pltpu.SemaphoreType.DMA((2 * GROUPS,)),
            pltpu.SemaphoreType.DMA((4,)),
            pltpu.SemaphoreType.DMA((4,)),
            pltpu.SemaphoreType.DMA((nx - 1,)),
            pltpu.SemaphoreType.DMA((nx - 1,)),
        ],
        compiler_params=pltpu.CompilerParams(
            collective_id=0, has_side_effects=True, vmem_limit_bytes=60 * 1024 * 1024
        ),
        cost_estimate=pl.CostEstimate(
            flops=16 * 2 * 128 * 256 * 256, bytes_accessed=8 * 1024 * 1024, transcendentals=0
        ),
    )(
        initial_warmth_field,
        horizontal_motion_pair,
        z_directed_motion,
        earlier_rate_change,
        layer_depth_spacing,
        backward_spread_ratio,
        wall_warmth_bounds,
    )


def solution(mesh):
    in_specs = (
        P(None, "gx", "gy"),
        P(None, None, "gx", "gy"),
        P(None, "gx", "gy"),
        P(None, "gx", "gy"),
        P(),
        P(),
        P(None, "gx", "gy"),
    )
    out_specs = (P(None, "gx", "gy"), P(None, "gx", "gy"))
    return jax.shard_map(
        on_device, mesh=mesh, in_specs=in_specs, out_specs=out_specs, check_vma=False
    )
```

```python
import functools

import jax
import jax.numpy as jnp
from jax import lax
from jax.experimental import pallas as pl
from jax.experimental.pallas import tpu as pltpu
from jax.sharding import PartitionSpec as P

COURANT = 0.5
DIFF_Y = 0.2
DIFF_Z = 0.25
NEW_TERM_COEF = 0.75
OLD_TERM_COEF = -5.0 / 12.0

MESH = pl.DeviceIdType.MESH
F32 = jnp.float32
BF16 = jnp.bfloat16
GROUPS = 4
OFF = 8


def each_level(start, stop, step, body, carry):
    def together(i, carry):
        for j in range(step):
            carry = body(start + i * step + j, carry)
        return carry

    return lax.fori_loop(0, (stop - start) // step, together, carry)


def lanes_of(shape):
    return lax.broadcasted_iota(jnp.int32, shape, len(shape) - 1)


def rows_of(shape):
    return lax.broadcasted_iota(jnp.int32, shape, len(shape) - 2)


def kernel(
    nx, ny, nz, m,
    t_hbm, uv_hbm, w_hbm, old_hbm, dz_hbm, r_hbm, wall_hbm,
    x_hbm, c_hbm,
    t, u_all, v_all, w, old, cur, rhs, green, head_pow, tail_pow, block_pow, far_block,
    theta, scale, inv_dz, up_coef, down_coef,
    pack, pack_got, edge, edge_got, edge_fix, side_fix, moment, moment_got, eights,
    dz_ref, r_ref,
    in_sem, out_sem, halo_send, halo_recv, moment_send, moment_recv,
):
    gx = lax.axis_index("gx")
    gy = lax.axis_index("gy")
    east, west = lax.rem(gx + 1, nx), lax.rem(gx + nx - 1, nx)
    north, south = lax.rem(gy + 1, ny), lax.rem(gy + ny - 1, ny)
    q_rows = m // 4
    blocks = m // 8
    inside = pl.ds(OFF, m)

    loads = [
        pltpu.make_async_copy(r_hbm, r_ref, in_sem.at[0]),
        pltpu.make_async_copy(dz_hbm, dz_ref, in_sem.at[1]),
        pltpu.make_async_copy(t_hbm, t.at[pl.ds(1, nz), inside], in_sem.at[2]),
        pltpu.make_async_copy(uv_hbm.at[1], v_all, in_sem.at[3]),
        pltpu.make_async_copy(uv_hbm.at[0], u_all.at[:, inside], in_sem.at[4]),
        pltpu.make_async_copy(wall_hbm.at[0], t.at[0, inside], in_sem.at[5]),
        pltpu.make_async_copy(wall_hbm.at[1], t.at[nz + 1, inside], in_sem.at[6]),
        pltpu.make_async_copy(w_hbm, w.at[pl.ds(1, nz)], in_sem.at[7]),
        pltpu.make_async_copy(old_hbm, old, in_sem.at[8]),
    ]
    for load in loads:
        load.start()

    barrier = pltpu.get_barrier_semaphore()
    for s in range(1, nx):
        pl.semaphore_signal(
            barrier, inc=1, device_id={"gx": lax.rem(gx + s, nx)}, device_id_type=MESH
        )
    for j in (north, south):
        pl.semaphore_signal(barrier, inc=1, device_id={"gy": j}, device_id_type=MESH)

    loads[0].wait()
    loads[1].wait()
    for k in range(nz):
        scale[k:k + 1, :] = jnp.full((1, m), r_ref[k], F32)
        inv_dz[k:k + 1, :] = 1.0 / jnp.full((1, m), dz_ref[k], F32)
    down_coef[0:1, :] = inv_dz[0:1, :]
    up_coef[nz - 1:nz, :] = inv_dz[nz - 1:nz, :]
    for k in range(nz - 1):
        between = 2.0 / jnp.full((1, m), dz_ref[k] + dz_ref[k + 1], F32)
        up_coef[k:k + 1, :] = between
        down_coef[k + 1:k + 2, :] = between
    up_coef[...] = DIFF_Z * up_coef[...] * inv_dz[...]
    down_coef[...] = DIFF_Z * down_coef[...] * inv_dz[...]
    inv_dz[...] = (-0.25 * COURANT) * inv_dz[...]
    r = scale[...]
    s = 0.5 / jnp.sqrt(r)
    theta[...] = 2.0 * jnp.log1p(s + s * s / (1.0 + jnp.sqrt(1.0 + s * s)))
    scale[...] = 1.0 / jnp.sqrt(1.0 + 4.0 * r)
    th = theta[...]
    for b in range(blocks):
        block_pow[b] = jnp.exp((-8.0 * b) * th)

    def make_tables(k, carry):
        row = rows_of((8, m))
        lane = lanes_of((8, m))
        th = theta[pl.ds(k, 1), :]
        head_pow[k] = jnp.exp(-th * row.astype(F32))
        tail_pow[k] = jnp.exp(-th * (7 - row).astype(F32))
        level_scale = scale[pl.ds(k, 1), :]
        near = level_scale * jnp.exp(-th * jnp.abs(row - lane).astype(F32))
        wrap = level_scale * jnp.exp(-th * (row - lane + m).astype(F32))
        for b in range(0, blocks, 2):
            full = jnp.concatenate(
                [
                    pltpu.roll(jnp.where(lane < m - 8 * c, near, wrap), 8 * c, 1)
                    if c
                    else near
                    for c in (b, b + 1)
                ],
                axis=0,
            )
            high = full.astype(BF16)
            green[k, 8 * b:8 * b + 16, 0:m] = high
            green[k, 8 * b:8 * b + 16, m:2 * m] = (full - high.astype(F32)).astype(BF16)
        return carry

    each_level(0, nz, 4, make_tables, 0)

    for load in loads[2:5]:
        load.wait()

    def make_pack(k, carry):
        pt, pv = carry
        pair = lanes_of((q_rows, m)) // 2
        for h in range(4):
            turn = 32 * h + 2 * k + 1
            mine = pair == 16 * h + k
            here = t[k + 1, OFF + h * q_rows:OFF + (h + 1) * q_rows, :]
            pt = jnp.where(mine, pltpu.roll(here, turn, 1), pt)
            pv = jnp.where(
                mine, pltpu.roll(v_all[k, h * q_rows:(h + 1) * q_rows, :], turn, 1), pv
            )
        edge[0, 0, pl.ds(k, 1), :] = t[k + 1, OFF + m - 1:OFF + m, :]
        edge[0, 1, pl.ds(k, 1), :] = u_all[k, OFF + m - 1:OFF + m, :]
        edge[1, 0, pl.ds(k, 1), :] = t[k + 1, OFF:OFF + 1, :]
        edge[1, 1, pl.ds(k, 1), :] = u_all[k, OFF:OFF + 1, :]
        return pt, pv

    blank = jnp.zeros((q_rows, m), F32)
    pt, pv = each_level(0, nz, 4, make_pack, (blank, blank))
    pack[0] = pt
    pack[1] = pv

    pl.semaphore_wait(barrier, nx + 1)

    def halo(src, dst, i, where):
        copy = pltpu.make_async_remote_copy(
            src_ref=src, dst_ref=dst, send_sem=halo_send.at[i], recv_sem=halo_recv.at[i],
            device_id=where, device_id_type=MESH,
        )
        copy.start()
        return copy

    halos = [
        halo(pack, pack_got.at[0], 0, {"gy": north}),
        halo(pack, pack_got.at[1], 1, {"gy": south}),
        halo(edge.at[0], edge_got.at[0], 2, {"gx": east}),
        halo(edge.at[1], edge_got.at[1], 3, {"gx": west}),
    ]

    for load in loads[5:]:
        load.wait()
    w[0] = -w[1]
    w[nz + 1] = -w[nz]

    def inner(k, carry):
        row = rows_of((q_rows, m))
        lane = lanes_of((q_rows, m))
        one = pl.ds(k, 1)
        up, down, idz = up_coef[one, :], down_coef[one, :], inv_dz[one, :]
        low_sum = jnp.zeros((8, m), F32)
        high_sum = jnp.zeros((8, m), F32)
        for h in range(4):
            rows = slice(h * q_rows, (h + 1) * q_rows)
            pad = slice(OFF + h * q_rows, OFF + (h + 1) * q_rows)
            after = slice(OFF + h * q_rows + 1, OFF + (h + 1) * q_rows + 1)
            before = slice(OFF + h * q_rows - 1, OFF + (h + 1) * q_rows - 1)
            here = t[k + 1, pad, :]
            u = u_all[k, pad, :]
            v = v_all[k, rows, :]
            fx = (u + u_all[k, after, :]) * (here + t[k + 1, after, :])
            gx_flux = (u_all[k, before, :] + u) * (t[k + 1, before, :] + here)
            if h == 3:
                fx = jnp.where(row == q_rows - 1, 0.0, fx)
            if h == 0:
                gx_flux = jnp.where(row == 0, 0.0, gx_flux)
            right = pltpu.roll(here, m - 1, 1)
            fy = (v + pltpu.roll(v, m - 1, 1)) * (here + right)
            fy = jnp.where(lane == m - 1, 0.0, fy)
            div = (fx - gx_flux) + (fy - pltpu.roll(fy, 1, 1))
            lap = jnp.where(lane == m - 1, 0.0, right) + jnp.where(
                lane == 0, 0.0, pltpu.roll(here, 1, 1)
            )
            below, above = t[k, pad, :], t[k + 2, pad, :]
            wk = w[k + 1, rows, :]
            fz = (wk + w[k + 2, rows, :]) * (here + above) - (w[k, rows, :] + wk) * (below + here)
            value = (
                (-0.25 * COURANT) * div
                + idz * fz
                + DIFF_Y * (lap - 2.0 * here)
                + (up * (above - here) - down * (here - below))
            )
            b = here + NEW_TERM_COEF * value + OLD_TERM_COEF * old[k, rows, :]
            cur[k, rows, :] = value
            rhs[k, rows, :] = b
            for i in range(4):
                c = 4 * h + i
                part = b[8 * i:8 * i + 8, :]
                low_sum = low_sum + block_pow[blocks - 1 - c, one, :] * part
                high_sum = high_sum + block_pow[c, one, :] * part
        eights[0, k] = tail_pow[k] * low_sum
        eights[1, k] = head_pow[k] * high_sum
        return carry

    each_level(0, nz, 2, inner, 0)

    lane1 = lanes_of((1, m))
    th_lane = jnp.zeros((1, m), F32)
    for k in range(nz):
        th_lane = jnp.where(lax.rem(lane1, 32) // 2 == k, theta[k:k + 1, :], th_lane)
    cell = rows_of((q_rows, m)) + (lanes_of((q_rows, m)) // 32) * q_rows
    weight_f = NEW_TERM_COEF * jnp.exp(-th_lane * cell.astype(F32))
    weight_g = NEW_TERM_COEF * jnp.exp(-th_lane * (m - 1 - cell).astype(F32))
    q_end = jnp.exp(-(m - 1.0) * th)
    sums_low = jnp.sum(eights[0], axis=1)
    sums_high = jnp.sum(eights[1], axis=1)

    for copy in halos:
        copy.wait_recv()

    first = lax.rem(lanes_of((q_rows, m)), 2) == 1
    near_t = jnp.where(
        first, pltpu.roll(pack_got[0, 0], 1, 1), pltpu.roll(pack_got[1, 0], m - 1, 1)
    )
    near_v = jnp.where(
        first, pltpu.roll(pack_got[0, 1], 1, 1), pltpu.roll(pack_got[1, 1], m - 1, 1)
    )
    flux = (pack[1] + near_v) * (pack[0] + near_t)
    fix = DIFF_Y * near_t + jnp.where(first, 0.25 * COURANT, -0.25 * COURANT) * flux
    side_fix[...] = fix
    low = (0.25 * COURANT) * (edge_got[0, 1] + edge[1, 1]) * (edge_got[0, 0] + edge[1, 0])
    top = (-0.25 * COURANT) * (edge_got[1, 1] + edge[0, 1]) * (edge_got[1, 0] + edge[0, 0])
    edge_fix[0] = low
    edge_fix[1] = top

    level = rows_of((nz, m))
    lane = lanes_of((nz, m))

    def spread(weights):
        line = jnp.sum(weights * fix, axis=0, keepdims=True)
        line = line + pltpu.roll(line, 32, 1)
        line = line + pltpu.roll(line, 64, 1)
        wide = jnp.broadcast_to(line, (nz, m))
        last = jnp.sum(jnp.where(lane == 2 * level, wide, 0.0), axis=1, keepdims=True)
        head = jnp.sum(jnp.where(lane == 2 * level + 1, wide, 0.0), axis=1, keepdims=True)
        return jnp.where(lane == 0, head, 0.0) + jnp.where(lane == m - 1, last, 0.0)

    moment[0] = sums_low + NEW_TERM_COEF * (q_end * low + top) + spread(weight_g)
    moment[1] = sums_high + NEW_TERM_COEF * (low + q_end * top) + spread(weight_f)

    sends = []
    for s in range(1, nx):
        copy = pltpu.make_async_remote_copy(
            src_ref=moment, dst_ref=moment_got.at[s - 1],
            send_sem=moment_send.at[s - 1], recv_sem=moment_recv.at[s - 1],
            device_id={"gx": lax.rem(gx + s, nx)}, device_id_type=MESH,
        )
        copy.start()
        sends.append(copy)

    def local_solve(k, carry):
        lane = lanes_of((q_rows, m))
        row = rows_of((q_rows, m))
        side = (lane == 0) | (lane == m - 1)
        parts = []
        for h in range(4):
            rows = slice(h * q_rows, (h + 1) * q_rows)
            extra = jnp.where(
                side, pltpu.roll(side_fix[...], m - 1 - 32 * h - 2 * k, 1), 0.0
            )
            if h == 0:
                extra = extra + jnp.where(row == 0, edge_fix[0, pl.ds(k, 1), :], 0.0)
            if h == 3:
                extra = extra + jnp.where(row == q_rows - 1, edge_fix[1, pl.ds(k, 1), :], 0.0)
            cur[k, rows, :] = cur[k, rows, :] + extra
            parts.append(rhs[k, rows, :] + NEW_TERM_COEF * extra)
        b = jnp.concatenate(parts, axis=0)
        high = b.astype(BF16)
        pair = jnp.concatenate([high, (b - high.astype(F32)).astype(BF16)], axis=1)
        both = jnp.dot(
            green[k], jnp.concatenate([pair, pair], axis=0), preferred_element_type=F32
        )
        rhs[k] = both[:, 0:m] + both[:, m:2 * m]
        return carry

    per = nz // GROUPS
    stores = []
    for part in range(GROUPS):
        each_level(part * per, (part + 1) * per, per, local_solve, 0)
        span = pl.ds(part * per, per)
        store = pltpu.make_async_copy(cur.at[span], c_hbm.at[span], out_sem.at[part])
        store.start()
        stores.append(store)

    step = jnp.exp(-float(m) * th)
    share = scale[...] * jnp.exp(-th) / (1.0 - jnp.exp(-float(m * nx) * th))
    powers = [jnp.ones_like(step)]
    for s in range(1, nx):
        powers.append(powers[-1] * step)
    from_low = powers[nx - 1] * moment[0]
    from_high = powers[nx - 1] * moment[1]

    for copy in sends:
        copy.wait_recv()
    for s in range(1, nx):
        from_low = from_low + powers[s - 1] * moment_got[s - 1, 0]
        from_high = from_high + powers[nx - s - 1] * moment_got[s - 1, 1]
    from_low = share * from_low
    from_high = share * from_high
    for b in range(blocks):
        far_block[0, b] = block_pow[b] * from_low
        far_block[1, b] = block_pow[blocks - 1 - b] * from_high

    def finish(k, carry):
        head = head_pow[k]
        tail = tail_pow[k]
        for b in range(blocks):
            rows = slice(8 * b, 8 * b + 8)
            rhs[k, rows, :] = (
                rhs[k, rows, :]
                + head * far_block[0, b, pl.ds(k, 1), :]
                + tail * far_block[1, b, pl.ds(k, 1), :]
            )
        return carry

    for part in range(GROUPS):
        each_level(part * per, (part + 1) * per, per, finish, 0)
        span = pl.ds(part * per, per)
        store = pltpu.make_async_copy(rhs.at[span], x_hbm.at[span], out_sem.at[GROUPS + part])
        store.start()
        stores.append(store)

    for copy in halos + sends:
        copy.wait_send()
    for store in stores:
        store.wait()


def on_device(
    initial_warmth_field,
    horizontal_motion_pair,
    z_directed_motion,
    earlier_rate_change,
    layer_depth_spacing,
    backward_spread_ratio,
    wall_warmth_bounds,
):
    nx = lax.axis_size("gx")
    ny = lax.axis_size("gy")
    nz, m, width = initial_warmth_field.shape
    assert nz == 16 and m == 128 and width == 128
    block = jax.ShapeDtypeStruct((nz, m, m), F32)
    anywhere = pl.BlockSpec(memory_space=pl.ANY)
    far_away = pl.BlockSpec(memory_space=pltpu.HBM)
    field = pltpu.VMEM((nz, m, m), F32)
    row = pltpu.VMEM((nz, m), F32)
    return pl.pallas_call(
        functools.partial(kernel, nx, ny, nz, m),
        out_shape=(block, block),
        in_specs=[far_away] * 7,
        out_specs=(anywhere, anywhere),
        scratch_shapes=[
            pltpu.VMEM((nz + 2, m + 2 * OFF, m), F32),
            pltpu.VMEM((nz, m + 2 * OFF, m), F32),
            field,
            pltpu.VMEM((nz + 2, m, m), F32),
            field, field, field,
            pltpu.VMEM((nz, m, 2 * m), BF16),
            pltpu.VMEM((nz, 8, m), F32),
            pltpu.VMEM((nz, 8, m), F32),
            pltpu.VMEM((m // 8, nz, m), F32),
            pltpu.VMEM((2, m // 8, nz, m), F32),
            row, row, row, row, row,
            pltpu.VMEM((2, m // 4, m), F32),
            pltpu.VMEM((2, 2, m // 4, m), F32),
            pltpu.VMEM((2, 2, nz, m), F32),
            pltpu.VMEM((2, 2, nz, m), F32),
            pltpu.VMEM((2, nz, m), F32),
            pltpu.VMEM((m // 4, m), F32),
            pltpu.VMEM((2, nz, m), F32),
            pltpu.VMEM((nx - 1, 2, nz, m), F32),
            pltpu.VMEM((2, nz, 8, m), F32),
            pltpu.SMEM((nz,), F32),
            pltpu.SMEM((nz,), F32),
            pltpu.SemaphoreType.DMA((9,)),
            pltpu.SemaphoreType.DMA((2 * GROUPS,)),
            pltpu.SemaphoreType.DMA((4,)),
            pltpu.SemaphoreType.DMA((4,)),
            pltpu.SemaphoreType.DMA((nx - 1,)),
            pltpu.SemaphoreType.DMA((nx - 1,)),
        ],
        compiler_params=pltpu.CompilerParams(
            collective_id=0, has_side_effects=True, vmem_limit_bytes=60 * 1024 * 1024
        ),
        cost_estimate=pl.CostEstimate(
            flops=16 * 2 * 128 * 256 * 256, bytes_accessed=8 * 1024 * 1024, transcendentals=0
        ),
    )(
        initial_warmth_field,
        horizontal_motion_pair,
        z_directed_motion,
        earlier_rate_change,
        layer_depth_spacing,
        backward_spread_ratio,
        wall_warmth_bounds,
    )


def solution(mesh):
    in_specs = (
        P(None, "gx", "gy"),
        P(None, None, "gx", "gy"),
        P(None, "gx", "gy"),
        P(None, "gx", "gy"),
        P(),
        P(),
        P(None, "gx", "gy"),
    )
    out_specs = (P(None, "gx", "gy"), P(None, "gx", "gy"))
    return jax.shard_map(
        on_device, mesh=mesh, in_specs=in_specs, out_specs=out_specs, check_vma=False
    )
```

```python
import functools

import jax
import jax.numpy as jnp
from jax import lax
from jax.experimental import pallas as pl
from jax.experimental.pallas import tpu as pltpu
from jax.sharding import PartitionSpec as P

COURANT = 0.5
DIFF_Y = 0.2
DIFF_Z = 0.25
NEW_TERM_COEF = 0.75
OLD_TERM_COEF = -5.0 / 12.0

MESH = pl.DeviceIdType.MESH
F32 = jnp.float32
BF16 = jnp.bfloat16
GROUPS = 4
OFF = 8


def each_level(start, stop, step, body, carry):
    def together(i, carry):
        for j in range(step):
            carry = body(start + i * step + j, carry)
        return carry

    return lax.fori_loop(0, (stop - start) // step, together, carry)


def lanes_of(shape):
    return lax.broadcasted_iota(jnp.int32, shape, len(shape) - 1)


def rows_of(shape):
    return lax.broadcasted_iota(jnp.int32, shape, len(shape) - 2)


def kernel(
    nx, ny, nz, m,
    t_hbm, uv_hbm, w_hbm, old_hbm, dz_hbm, r_hbm, wall_hbm,
    rhs, cur, head_pow, tail_pow, far_block,
    t, u_all, v_all, w, old, green, block_pow,
    theta, scale, inv_dz, up_coef, down_coef,
    pack, pack_got, edge, edge_got, edge_fix, side_fix, moment, moment_got, eights,
    dz_ref, r_ref,
    in_sem, halo_send, halo_recv, moment_send, moment_recv,
):
    gx = lax.axis_index("gx")
    gy = lax.axis_index("gy")
    east, west = lax.rem(gx + 1, nx), lax.rem(gx + nx - 1, nx)
    north, south = lax.rem(gy + 1, ny), lax.rem(gy + ny - 1, ny)
    q_rows = m // 4
    blocks = m // 8
    inside = pl.ds(OFF, m)

    loads = [
        pltpu.make_async_copy(r_hbm, r_ref, in_sem.at[0]),
        pltpu.make_async_copy(dz_hbm, dz_ref, in_sem.at[1]),
        pltpu.make_async_copy(t_hbm, t.at[pl.ds(1, nz), inside], in_sem.at[2]),
        pltpu.make_async_copy(uv_hbm.at[1], v_all, in_sem.at[3]),
        pltpu.make_async_copy(uv_hbm.at[0], u_all.at[:, inside], in_sem.at[4]),
        pltpu.make_async_copy(wall_hbm.at[0], t.at[0, inside], in_sem.at[5]),
        pltpu.make_async_copy(wall_hbm.at[1], t.at[nz + 1, inside], in_sem.at[6]),
        pltpu.make_async_copy(w_hbm, w.at[pl.ds(1, nz)], in_sem.at[7]),
        pltpu.make_async_copy(old_hbm, old, in_sem.at[8]),
    ]
    for load in loads:
        load.start()

    barrier = pltpu.get_barrier_semaphore()
    for s in range(1, nx):
        pl.semaphore_signal(
            barrier, inc=1, device_id={"gx": lax.rem(gx + s, nx)}, device_id_type=MESH
        )
    for j in (north, south):
        pl.semaphore_signal(barrier, inc=1, device_id={"gy": j}, device_id_type=MESH)

    loads[0].wait()
    loads[1].wait()
    for k in range(nz):
        scale[k:k + 1, :] = jnp.full((1, m), r_ref[k], F32)
        inv_dz[k:k + 1, :] = 1.0 / jnp.full((1, m), dz_ref[k], F32)
    down_coef[0:1, :] = inv_dz[0:1, :]
    up_coef[nz - 1:nz, :] = inv_dz[nz - 1:nz, :]
    for k in range(nz - 1):
        between = 2.0 / jnp.full((1, m), dz_ref[k] + dz_ref[k + 1], F32)
        up_coef[k:k + 1, :] = between
        down_coef[k + 1:k + 2, :] = between
    up_coef[...] = DIFF_Z * up_coef[...] * inv_dz[...]
    down_coef[...] = DIFF_Z * down_coef[...] * inv_dz[...]
    inv_dz[...] = (-0.25 * COURANT) * inv_dz[...]
    r = scale[...]
    s = 0.5 / jnp.sqrt(r)
    theta[...] = 2.0 * jnp.log1p(s + s * s / (1.0 + jnp.sqrt(1.0 + s * s)))
    scale[...] = 1.0 / jnp.sqrt(1.0 + 4.0 * r)
    th = theta[...]
    for b in range(blocks):
        block_pow[b] = jnp.exp((-8.0 * b) * th)

    def make_tables(k, carry):
        row = rows_of((8, m))
        lane = lanes_of((8, m))
        th = theta[pl.ds(k, 1), :]
        head_pow[k] = jnp.exp(-th * row.astype(F32))
        tail_pow[k] = jnp.exp(-th * (7 - row).astype(F32))
        level_scale = scale[pl.ds(k, 1), :]
        near = level_scale * jnp.exp(-th * jnp.abs(row - lane).astype(F32))
        wrap = level_scale * jnp.exp(-th * (row - lane + m).astype(F32))
        for b in range(0, blocks, 2):
            full = jnp.concatenate(
                [
                    pltpu.roll(jnp.where(lane < m - 8 * c, near, wrap), 8 * c, 1)
                    if c
                    else near
                    for c in (b, b + 1)
                ],
                axis=0,
            )
            high = full.astype(BF16)
            green[k, 8 * b:8 * b + 16, 0:m] = high
            green[k, 8 * b:8 * b + 16, m:2 * m] = (full - high.astype(F32)).astype(BF16)
        return carry

    each_level(0, nz, 4, make_tables, 0)

    for load in loads[2:5]:
        load.wait()

    def make_pack(k, carry):
        pt, pv = carry
        pair = lanes_of((q_rows, m)) // 2
        for h in range(4):
            turn = 32 * h + 2 * k + 1
            mine = pair == 16 * h + k
            here = t[k + 1, OFF + h * q_rows:OFF + (h + 1) * q_rows, :]
            pt = jnp.where(mine, pltpu.roll(here, turn, 1), pt)
            pv = jnp.where(
                mine, pltpu.roll(v_all[k, h * q_rows:(h + 1) * q_rows, :], turn, 1), pv
            )
        edge[0, 0, pl.ds(k, 1), :] = t[k + 1, OFF + m - 1:OFF + m, :]
        edge[0, 1, pl.ds(k, 1), :] = u_all[k, OFF + m - 1:OFF + m, :]
        edge[1, 0, pl.ds(k, 1), :] = t[k + 1, OFF:OFF + 1, :]
        edge[1, 1, pl.ds(k, 1), :] = u_all[k, OFF:OFF + 1, :]
        return pt, pv

    blank = jnp.zeros((q_rows, m), F32)
    pt, pv = each_level(0, nz, 4, make_pack, (blank, blank))
    pack[0] = pt
    pack[1] = pv

    pl.semaphore_wait(barrier, nx + 1)

    def halo(src, dst, i, where):
        copy = pltpu.make_async_remote_copy(
            src_ref=src, dst_ref=dst, send_sem=halo_send.at[i], recv_sem=halo_recv.at[i],
            device_id=where, device_id_type=MESH,
        )
        copy.start()
        return copy

    halos = [
        halo(pack, pack_got.at[0], 0, {"gy": north}),
        halo(pack, pack_got.at[1], 1, {"gy": south}),
        halo(edge.at[0], edge_got.at[0], 2, {"gx": east}),
        halo(edge.at[1], edge_got.at[1], 3, {"gx": west}),
    ]

    for load in loads[5:]:
        load.wait()
    w[0] = -w[1]
    w[nz + 1] = -w[nz]

    def inner(k, carry):
        row = rows_of((q_rows, m))
        lane = lanes_of((q_rows, m))
        one = pl.ds(k, 1)
        up, down, idz = up_coef[one, :], down_coef[one, :], inv_dz[one, :]
        low_sum = jnp.zeros((8, m), F32)
        high_sum = jnp.zeros((8, m), F32)
        for h in range(4):
            rows = slice(h * q_rows, (h + 1) * q_rows)
            pad = slice(OFF + h * q_rows, OFF + (h + 1) * q_rows)
            after = slice(OFF + h * q_rows + 1, OFF + (h + 1) * q_rows + 1)
            before = slice(OFF + h * q_rows - 1, OFF + (h + 1) * q_rows - 1)
            here = t[k + 1, pad, :]
            u = u_all[k, pad, :]
            v = v_all[k, rows, :]
            fx = (u + u_all[k, after, :]) * (here + t[k + 1, after, :])
            gx_flux = (u_all[k, before, :] + u) * (t[k + 1, before, :] + here)
            if h == 3:
                fx = jnp.where(row == q_rows - 1, 0.0, fx)
            if h == 0:
                gx_flux = jnp.where(row == 0, 0.0, gx_flux)
            right = pltpu.roll(here, m - 1, 1)
            fy = (v + pltpu.roll(v, m - 1, 1)) * (here + right)
            fy = jnp.where(lane == m - 1, 0.0, fy)
            div = (fx - gx_flux) + (fy - pltpu.roll(fy, 1, 1))
            lap = jnp.where(lane == m - 1, 0.0, right) + jnp.where(
                lane == 0, 0.0, pltpu.roll(here, 1, 1)
            )
            below, above = t[k, pad, :], t[k + 2, pad, :]
            wk = w[k + 1, rows, :]
            fz = (wk + w[k + 2, rows, :]) * (here + above) - (w[k, rows, :] + wk) * (below + here)
            value = (
                (-0.25 * COURANT) * div
                + idz * fz
                + DIFF_Y * (lap - 2.0 * here)
                + (up * (above - here) - down * (here - below))
            )
            b = here + NEW_TERM_COEF * value + OLD_TERM_COEF * old[k, rows, :]
            cur[k, rows, :] = value
            rhs[k, rows, :] = b
            for i in range(4):
                c = 4 * h + i
                part = b[8 * i:8 * i + 8, :]
                low_sum = low_sum + block_pow[blocks - 1 - c, one, :] * part
                high_sum = high_sum + block_pow[c, one, :] * part
        eights[0, k] = tail_pow[k] * low_sum
        eights[1, k] = head_pow[k] * high_sum
        return carry

    each_level(0, nz, 2, inner, 0)

    lane1 = lanes_of((1, m))
    th_lane = jnp.zeros((1, m), F32)
    for k in range(nz):
        th_lane = jnp.where(lax.rem(lane1, 32) // 2 == k, theta[k:k + 1, :], th_lane)
    cell = rows_of((q_rows, m)) + (lanes_of((q_rows, m)) // 32) * q_rows
    weight_f = NEW_TERM_COEF * jnp.exp(-th_lane * cell.astype(F32))
    weight_g = NEW_TERM_COEF * jnp.exp(-th_lane * (m - 1 - cell).astype(F32))
    q_end = jnp.exp(-(m - 1.0) * th)
    sums_low = jnp.sum(eights[0], axis=1)
    sums_high = jnp.sum(eights[1], axis=1)

    for copy in halos:
        copy.wait_recv()

    first = lax.rem(lanes_of((q_rows, m)), 2) == 1
    near_t = jnp.where(
        first, pltpu.roll(pack_got[0, 0], 1, 1), pltpu.roll(pack_got[1, 0], m - 1, 1)
    )
    near_v = jnp.where(
        first, pltpu.roll(pack_got[0, 1], 1, 1), pltpu.roll(pack_got[1, 1], m - 1, 1)
    )
    flux = (pack[1] + near_v) * (pack[0] + near_t)
    fix = DIFF_Y * near_t + jnp.where(first, 0.25 * COURANT, -0.25 * COURANT) * flux
    side_fix[...] = fix
    low = (0.25 * COURANT) * (edge_got[0, 1] + edge[1, 1]) * (edge_got[0, 0] + edge[1, 0])
    top = (-0.25 * COURANT) * (edge_got[1, 1] + edge[0, 1]) * (edge_got[1, 0] + edge[0, 0])
    edge_fix[0] = low
    edge_fix[1] = top

    level = rows_of((nz, m))
    lane = lanes_of((nz, m))

    def spread(weights):
        line = jnp.sum(weights * fix, axis=0, keepdims=True)
        line = line + pltpu.roll(line, 32, 1)
        line = line + pltpu.roll(line, 64, 1)
        wide = jnp.broadcast_to(line, (nz, m))
        last = jnp.sum(jnp.where(lane == 2 * level, wide, 0.0), axis=1, keepdims=True)
        head = jnp.sum(jnp.where(lane == 2 * level + 1, wide, 0.0), axis=1, keepdims=True)
        return jnp.where(lane == 0, head, 0.0) + jnp.where(lane == m - 1, last, 0.0)

    moment[0] = sums_low + NEW_TERM_COEF * (q_end * low + top) + spread(weight_g)
    moment[1] = sums_high + NEW_TERM_COEF * (low + q_end * top) + spread(weight_f)

    sends = []
    for s in range(1, nx):
        copy = pltpu.make_async_remote_copy(
            src_ref=moment, dst_ref=moment_got.at[s - 1],
            send_sem=moment_send.at[s - 1], recv_sem=moment_recv.at[s - 1],
            device_id={"gx": lax.rem(gx + s, nx)}, device_id_type=MESH,
        )
        copy.start()
        sends.append(copy)

    def local_solve(k, carry):
        lane = lanes_of((q_rows, m))
        row = rows_of((q_rows, m))
        side = (lane == 0) | (lane == m - 1)
        parts = []
        for h in range(4):
            rows = slice(h * q_rows, (h + 1) * q_rows)
            extra = jnp.where(
                side, pltpu.roll(side_fix[...], m - 1 - 32 * h - 2 * k, 1), 0.0
            )
            if h == 0:
                extra = extra + jnp.where(row == 0, edge_fix[0, pl.ds(k, 1), :], 0.0)
            if h == 3:
                extra = extra + jnp.where(row == q_rows - 1, edge_fix[1, pl.ds(k, 1), :], 0.0)
            cur[k, rows, :] = cur[k, rows, :] + extra
            parts.append(rhs[k, rows, :] + NEW_TERM_COEF * extra)
        b = jnp.concatenate(parts, axis=0)
        high = b.astype(BF16)
        pair = jnp.concatenate([high, (b - high.astype(F32)).astype(BF16)], axis=1)
        both = jnp.dot(
            green[k], jnp.concatenate([pair, pair], axis=0), preferred_element_type=F32
        )
        rhs[k] = both[:, 0:m] + both[:, m:2 * m]
        return carry

    each_level(0, nz, 4, local_solve, 0)

    step = jnp.exp(-float(m) * th)
    share = scale[...] * jnp.exp(-th) / (1.0 - jnp.exp(-float(m * nx) * th))
    powers = [jnp.ones_like(step)]
    for s in range(1, nx):
        powers.append(powers[-1] * step)
    from_low = powers[nx - 1] * moment[0]
    from_high = powers[nx - 1] * moment[1]

    for copy in sends:
        copy.wait_recv()
    for s in range(1, nx):
        from_low = from_low + powers[s - 1] * moment_got[s - 1, 0]
        from_high = from_high + powers[nx - s - 1] * moment_got[s - 1, 1]
    from_low = share * from_low
    from_high = share * from_high
    for b in range(blocks):
        far_block[0, b] = block_pow[b] * from_low
        far_block[1, b] = block_pow[blocks - 1 - b] * from_high

    for copy in halos + sends:
        copy.wait_send()


def finish_kernel(nz, m, part_ref, cur_ref, head_pow, tail_pow, far_block, x_hbm, c_hbm, x, out_sem):
    blocks = m // 8
    stores = [pltpu.make_async_copy(cur_ref, c_hbm, out_sem.at[GROUPS])]
    stores[0].start()

    def finish(k, carry):
        head = head_pow[k]
        tail = tail_pow[k]
        for b in range(blocks):
            rows = slice(8 * b, 8 * b + 8)
            x[k, rows, :] = (
                part_ref[k, rows, :]
                + head * far_block[0, b, pl.ds(k, 1), :]
                + tail * far_block[1, b, pl.ds(k, 1), :]
            )
        return carry

    per = nz // GROUPS
    for part in range(GROUPS):
        each_level(part * per, (part + 1) * per, per, finish, 0)
        span = pl.ds(part * per, per)
        store = pltpu.make_async_copy(x.at[span], x_hbm.at[span], out_sem.at[part])
        store.start()
        stores.append(store)
    for store in stores:
        store.wait()


def on_device(
    initial_warmth_field,
    horizontal_motion_pair,
    z_directed_motion,
    earlier_rate_change,
    layer_depth_spacing,
    backward_spread_ratio,
    wall_warmth_bounds,
):
    nx = lax.axis_size("gx")
    ny = lax.axis_size("gy")
    nz, m, width = initial_warmth_field.shape
    assert nz == 16 and m == 128 and width == 128
    block = jax.ShapeDtypeStruct((nz, m, m), F32)
    anywhere = pl.BlockSpec(memory_space=pl.ANY)
    far_away = pl.BlockSpec(memory_space=pltpu.HBM)
    field = pltpu.VMEM((nz, m, m), F32)
    row = pltpu.VMEM((nz, m), F32)
    near = pl.BlockSpec(memory_space=pltpu.VMEM)
    carried = (
        field,
        field,
        pltpu.VMEM((nz, 8, m), F32),
        pltpu.VMEM((nz, 8, m), F32),
        pltpu.VMEM((2, m // 8, nz, m), F32),
    )
    between = pl.pallas_call(
        functools.partial(kernel, nx, ny, nz, m),
        out_shape=carried,
        in_specs=[far_away] * 7,
        out_specs=(near,) * 5,
        scratch_shapes=[
            pltpu.VMEM((nz + 2, m + 2 * OFF, m), F32),
            pltpu.VMEM((nz, m + 2 * OFF, m), F32),
            field,
            pltpu.VMEM((nz + 2, m, m), F32),
            field,
            pltpu.VMEM((nz, m, 2 * m), BF16),
            pltpu.VMEM((m // 8, nz, m), F32),
            row, row, row, row, row,
            pltpu.VMEM((2, m // 4, m), F32),
            pltpu.VMEM((2, 2, m // 4, m), F32),
            pltpu.VMEM((2, 2, nz, m), F32),
            pltpu.VMEM((2, 2, nz, m), F32),
            pltpu.VMEM((2, nz, m), F32),
            pltpu.VMEM((m // 4, m), F32),
            pltpu.VMEM((2, nz, m), F32),
            pltpu.VMEM((nx - 1, 2, nz, m), F32),
            pltpu.VMEM((2, nz, 8, m), F32),
            pltpu.SMEM((nz,), F32),
            pltpu.SMEM((nz,), F32),
            pltpu.SemaphoreType.DMA((9,)),
            pltpu.SemaphoreType.DMA((4,)),
            pltpu.SemaphoreType.DMA((4,)),
            pltpu.SemaphoreType.DMA((nx - 1,)),
            pltpu.SemaphoreType.DMA((nx - 1,)),
        ],
        compiler_params=pltpu.CompilerParams(
            collective_id=0, has_side_effects=True, vmem_limit_bytes=58 * 1024 * 1024
        ),
        cost_estimate=pl.CostEstimate(
            flops=16 * 2 * 128 * 256 * 256, bytes_accessed=8 * 1024 * 1024, transcendentals=0
        ),
    )(
        initial_warmth_field,
        horizontal_motion_pair,
        z_directed_motion,
        earlier_rate_change,
        layer_depth_spacing,
        backward_spread_ratio,
        wall_warmth_bounds,
    )
    return pl.pallas_call(
        functools.partial(finish_kernel, nz, m),
        out_shape=(block, block),
        in_specs=[near] * 5,
        out_specs=(anywhere, anywhere),
        scratch_shapes=[field, pltpu.SemaphoreType.DMA((GROUPS + 1,))],
        compiler_params=pltpu.CompilerParams(vmem_limit_bytes=16 * 1024 * 1024),
    )(*between)


def solution(mesh):
    in_specs = (
        P(None, "gx", "gy"),
        P(None, None, "gx", "gy"),
        P(None, "gx", "gy"),
        P(None, "gx", "gy"),
        P(),
        P(),
        P(None, "gx", "gy"),
    )
    out_specs = (P(None, "gx", "gy"), P(None, "gx", "gy"))
    return jax.shard_map(
        on_device, mesh=mesh, in_specs=in_specs, out_specs=out_specs, check_vma=False
    )
```

```python
import functools

import jax
import jax.numpy as jnp
from jax import lax
from jax.experimental import pallas as pl
from jax.experimental.pallas import tpu as pltpu
from jax.sharding import PartitionSpec as P

COURANT = 0.5
DIFF_Y = 0.2
DIFF_Z = 0.25
NEW_TERM_COEF = 0.75
OLD_TERM_COEF = -5.0 / 12.0

MESH = pl.DeviceIdType.MESH
F32 = jnp.float32
BF16 = jnp.bfloat16
GROUPS = 4
OFF = 8


def each_level(start, stop, step, body, carry):
    def together(i, carry):
        for j in range(step):
            carry = body(start + i * step + j, carry)
        return carry

    return lax.fori_loop(0, (stop - start) // step, together, carry)


def lanes_of(shape):
    return lax.broadcasted_iota(jnp.int32, shape, len(shape) - 1)


def rows_of(shape):
    return lax.broadcasted_iota(jnp.int32, shape, len(shape) - 2)


def kernel(
    nx, ny, nz, m,
    t_hbm, uv_hbm, w_hbm, old_hbm, dz_hbm, r_hbm, wall_hbm,
    rhs, cur, head_pow, tail_pow, far_block,
    t, u_all, v_all, w, old, green, block_pow,
    theta, scale, inv_dz, up_coef, down_coef,
    pack, pack_got, edge, edge_got, edge_fix, side_fix, moment, moment_got, eights,
    dz_ref, r_ref,
    in_sem, halo_send, halo_recv, moment_send, moment_recv,
):
    gx = lax.axis_index("gx")
    gy = lax.axis_index("gy")
    east, west = lax.rem(gx + 1, nx), lax.rem(gx + nx - 1, nx)
    north, south = lax.rem(gy + 1, ny), lax.rem(gy + ny - 1, ny)
    q_rows = m // 4
    blocks = m // 8
    inside = pl.ds(OFF, m)

    loads = [
        pltpu.make_async_copy(r_hbm, r_ref, in_sem.at[0]),
        pltpu.make_async_copy(dz_hbm, dz_ref, in_sem.at[1]),
        pltpu.make_async_copy(t_hbm, t.at[pl.ds(1, nz), inside], in_sem.at[2]),
        pltpu.make_async_copy(uv_hbm.at[1], v_all, in_sem.at[3]),
        pltpu.make_async_copy(uv_hbm.at[0], u_all.at[:, inside], in_sem.at[4]),
        pltpu.make_async_copy(wall_hbm.at[0], t.at[0, inside], in_sem.at[5]),
        pltpu.make_async_copy(wall_hbm.at[1], t.at[nz + 1, inside], in_sem.at[6]),
        pltpu.make_async_copy(w_hbm, w.at[pl.ds(1, nz)], in_sem.at[7]),
        pltpu.make_async_copy(old_hbm, old, in_sem.at[8]),
    ]
    for load in loads:
        load.start()

    barrier = pltpu.get_barrier_semaphore()
    for s in range(1, nx):
        pl.semaphore_signal(
            barrier, inc=1, device_id={"gx": lax.rem(gx + s, nx)}, device_id_type=MESH
        )
    for j in (north, south):
        pl.semaphore_signal(barrier, inc=1, device_id={"gy": j}, device_id_type=MESH)

    for load in loads[2:5]:
        load.wait()

    def make_pack(k, carry):
        pt, pv = carry
        pair = lanes_of((q_rows, m)) // 2
        for h in range(4):
            turn = 32 * h + 2 * k + 1
            mine = pair == 16 * h + k
            here = t[k + 1, OFF + h * q_rows:OFF + (h + 1) * q_rows, :]
            pt = jnp.where(mine, pltpu.roll(here, turn, 1), pt)
            pv = jnp.where(
                mine, pltpu.roll(v_all[k, h * q_rows:(h + 1) * q_rows, :], turn, 1), pv
            )
        edge[0, 0, pl.ds(k, 1), :] = t[k + 1, OFF + m - 1:OFF + m, :]
        edge[0, 1, pl.ds(k, 1), :] = u_all[k, OFF + m - 1:OFF + m, :]
        edge[1, 0, pl.ds(k, 1), :] = t[k + 1, OFF:OFF + 1, :]
        edge[1, 1, pl.ds(k, 1), :] = u_all[k, OFF:OFF + 1, :]
        return pt, pv

    blank = jnp.zeros((q_rows, m), F32)
    pt, pv = each_level(0, nz, 4, make_pack, (blank, blank))
    pack[0] = pt
    pack[1] = pv

    pl.semaphore_wait(barrier, nx + 1)

    def halo(src, dst, i, where):
        copy = pltpu.make_async_remote_copy(
            src_ref=src, dst_ref=dst, send_sem=halo_send.at[i], recv_sem=halo_recv.at[i],
            device_id=where, device_id_type=MESH,
        )
        copy.start()
        return copy

    halos = [
        halo(pack, pack_got.at[0], 0, {"gy": north}),
        halo(pack, pack_got.at[1], 1, {"gy": south}),
        halo(edge.at[0], edge_got.at[0], 2, {"gx": east}),
        halo(edge.at[1], edge_got.at[1], 3, {"gx": west}),
    ]

    loads[0].wait()
    loads[1].wait()
    for k in range(nz):
        scale[k:k + 1, :] = jnp.full((1, m), r_ref[k], F32)
        inv_dz[k:k + 1, :] = 1.0 / jnp.full((1, m), dz_ref[k], F32)
    down_coef[0:1, :] = inv_dz[0:1, :]
    up_coef[nz - 1:nz, :] = inv_dz[nz - 1:nz, :]
    for k in range(nz - 1):
        between = 2.0 / jnp.full((1, m), dz_ref[k] + dz_ref[k + 1], F32)
        up_coef[k:k + 1, :] = between
        down_coef[k + 1:k + 2, :] = between
    up_coef[...] = DIFF_Z * up_coef[...] * inv_dz[...]
    down_coef[...] = DIFF_Z * down_coef[...] * inv_dz[...]
    inv_dz[...] = (-0.25 * COURANT) * inv_dz[...]
    r = scale[...]
    s = 0.5 / jnp.sqrt(r)
    theta[...] = 2.0 * jnp.log1p(s + s * s / (1.0 + jnp.sqrt(1.0 + s * s)))
    scale[...] = 1.0 / jnp.sqrt(1.0 + 4.0 * r)
    th = theta[...]
    for b in range(blocks):
        block_pow[b] = jnp.exp((-8.0 * b) * th)

    def make_tables(k, carry):
        row = rows_of((8, m))
        lane = lanes_of((8, m))
        th = theta[pl.ds(k, 1), :]
        head_pow[k] = jnp.exp(-th * row.astype(F32))
        tail_pow[k] = jnp.exp(-th * (7 - row).astype(F32))
        return carry

    each_level(0, nz, 4, make_tables, 0)

    for load in loads[5:]:
        load.wait()
    w[0] = -w[1]
    w[nz + 1] = -w[nz]

    def inner(k, carry):
        row = rows_of((q_rows, m))
        lane = lanes_of((q_rows, m))
        one = pl.ds(k, 1)
        up, down, idz = up_coef[one, :], down_coef[one, :], inv_dz[one, :]
        low_sum = jnp.zeros((8, m), F32)
        high_sum = jnp.zeros((8, m), F32)
        for h in range(4):
            rows = slice(h * q_rows, (h + 1) * q_rows)
            pad = slice(OFF + h * q_rows, OFF + (h + 1) * q_rows)
            after = slice(OFF + h * q_rows + 1, OFF + (h + 1) * q_rows + 1)
            before = slice(OFF + h * q_rows - 1, OFF + (h + 1) * q_rows - 1)
            here = t[k + 1, pad, :]
            u = u_all[k, pad, :]
            v = v_all[k, rows, :]
            fx = (u + u_all[k, after, :]) * (here + t[k + 1, after, :])
            gx_flux = (u_all[k, before, :] + u) * (t[k + 1, before, :] + here)
            if h == 3:
                fx = jnp.where(row == q_rows - 1, 0.0, fx)
            if h == 0:
                gx_flux = jnp.where(row == 0, 0.0, gx_flux)
            right = pltpu.roll(here, m - 1, 1)
            fy = (v + pltpu.roll(v, m - 1, 1)) * (here + right)
            fy = jnp.where(lane == m - 1, 0.0, fy)
            div = (fx - gx_flux) + (fy - pltpu.roll(fy, 1, 1))
            lap = jnp.where(lane == m - 1, 0.0, right) + jnp.where(
                lane == 0, 0.0, pltpu.roll(here, 1, 1)
            )
            below, above = t[k, pad, :], t[k + 2, pad, :]
            wk = w[k + 1, rows, :]
            fz = (wk + w[k + 2, rows, :]) * (here + above) - (w[k, rows, :] + wk) * (below + here)
            value = (
                (-0.25 * COURANT) * div
                + idz * fz
                + DIFF_Y * (lap - 2.0 * here)
                + (up * (above - here) - down * (here - below))
            )
            b = here + NEW_TERM_COEF * value + OLD_TERM_COEF * old[k, rows, :]
            cur[k, rows, :] = value
            rhs[k, rows, :] = b
            for i in range(4):
                c = 4 * h + i
                part = b[8 * i:8 * i + 8, :]
                low_sum = low_sum + block_pow[blocks - 1 - c, one, :] * part
                high_sum = high_sum + block_pow[c, one, :] * part
        eights[0, k] = tail_pow[k] * low_sum
        eights[1, k] = head_pow[k] * high_sum
        return carry

    each_level(0, nz, 4, inner, 0)

    lane1 = lanes_of((1, m))
    th_lane = jnp.zeros((1, m), F32)
    for k in range(nz):
        th_lane = jnp.where(lax.rem(lane1, 32) // 2 == k, theta[k:k + 1, :], th_lane)
    cell = rows_of((q_rows, m)) + (lanes_of((q_rows, m)) // 32) * q_rows
    weight_f = NEW_TERM_COEF * jnp.exp(-th_lane * cell.astype(F32))
    weight_g = NEW_TERM_COEF * jnp.exp(-th_lane * (m - 1 - cell).astype(F32))
    q_end = jnp.exp(-(m - 1.0) * th)
    sums_low = jnp.sum(eights[0], axis=1)
    sums_high = jnp.sum(eights[1], axis=1)

    for copy in halos:
        copy.wait_recv()

    first = lax.rem(lanes_of((q_rows, m)), 2) == 1
    near_t = jnp.where(
        first, pltpu.roll(pack_got[0, 0], 1, 1), pltpu.roll(pack_got[1, 0], m - 1, 1)
    )
    near_v = jnp.where(
        first, pltpu.roll(pack_got[0, 1], 1, 1), pltpu.roll(pack_got[1, 1], m - 1, 1)
    )
    flux = (pack[1] + near_v) * (pack[0] + near_t)
    fix = DIFF_Y * near_t + jnp.where(first, 0.25 * COURANT, -0.25 * COURANT) * flux
    side_fix[...] = fix
    low = (0.25 * COURANT) * (edge_got[0, 1] + edge[1, 1]) * (edge_got[0, 0] + edge[1, 0])
    top = (-0.25 * COURANT) * (edge_got[1, 1] + edge[0, 1]) * (edge_got[1, 0] + edge[0, 0])
    edge_fix[0] = low
    edge_fix[1] = top

    level = rows_of((nz, m))
    lane = lanes_of((nz, m))

    def spread(weights):
        line = jnp.sum(weights * fix, axis=0, keepdims=True)
        line = line + pltpu.roll(line, 32, 1)
        line = line + pltpu.roll(line, 64, 1)
        wide = jnp.broadcast_to(line, (nz, m))
        last = jnp.sum(jnp.where(lane == 2 * level, wide, 0.0), axis=1, keepdims=True)
        head = jnp.sum(jnp.where(lane == 2 * level + 1, wide, 0.0), axis=1, keepdims=True)
        return jnp.where(lane == 0, head, 0.0) + jnp.where(lane == m - 1, last, 0.0)

    moment[0] = sums_low + NEW_TERM_COEF * (q_end * low + top) + spread(weight_g)
    moment[1] = sums_high + NEW_TERM_COEF * (low + q_end * top) + spread(weight_f)

    sends = []
    for s in range(1, nx):
        copy = pltpu.make_async_remote_copy(
            src_ref=moment, dst_ref=moment_got.at[s - 1],
            send_sem=moment_send.at[s - 1], recv_sem=moment_recv.at[s - 1],
            device_id={"gx": lax.rem(gx + s, nx)}, device_id_type=MESH,
        )
        copy.start()
        sends.append(copy)

    def local_inverse(k, carry):
        row8 = rows_of((8, m))
        lane8 = lanes_of((8, m))
        th = theta[pl.ds(k, 1), :]
        level_scale = scale[pl.ds(k, 1), :]
        near = level_scale * jnp.exp(-th * jnp.abs(row8 - lane8).astype(F32))
        wrap = level_scale * jnp.exp(-th * (row8 - lane8 + m).astype(F32))
        for b0 in range(0, blocks, 2):
            full = jnp.concatenate(
                [
                    pltpu.roll(jnp.where(lane8 < m - 8 * c, near, wrap), 8 * c, 1)
                    if c
                    else near
                    for c in (b0, b0 + 1)
                ],
                axis=0,
            )
            high = full.astype(BF16)
            green[k, 8 * b0:8 * b0 + 16, 0:m] = high
            green[k, 8 * b0:8 * b0 + 16, m:2 * m] = (full - high.astype(F32)).astype(BF16)
        return carry

    each_level(0, nz, 4, local_inverse, 0)

    def local_solve(k, carry):
        lane = lanes_of((q_rows, m))
        row = rows_of((q_rows, m))
        side = (lane == 0) | (lane == m - 1)
        parts = []
        for h in range(4):
            rows = slice(h * q_rows, (h + 1) * q_rows)
            extra = jnp.where(
                side, pltpu.roll(side_fix[...], m - 1 - 32 * h - 2 * k, 1), 0.0
            )
            if h == 0:
                extra = extra + jnp.where(row == 0, edge_fix[0, pl.ds(k, 1), :], 0.0)
            if h == 3:
                extra = extra + jnp.where(row == q_rows - 1, edge_fix[1, pl.ds(k, 1), :], 0.0)
            cur[k, rows, :] = cur[k, rows, :] + extra
            parts.append(rhs[k, rows, :] + NEW_TERM_COEF * extra)
        b = jnp.concatenate(parts, axis=0)
        high = b.astype(BF16)
        pair = jnp.concatenate([high, (b - high.astype(F32)).astype(BF16)], axis=1)
        both = jnp.dot(
            green[k], jnp.concatenate([pair, pair], axis=0), preferred_element_type=F32
        )
        rhs[k] = both[:, 0:m] + both[:, m:2 * m]
        return carry

    each_level(0, nz, 4, local_solve, 0)

    step = jnp.exp(-float(m) * th)
    share = scale[...] * jnp.exp(-th) / (1.0 - jnp.exp(-float(m * nx) * th))
    powers = [jnp.ones_like(step)]
    for s in range(1, nx):
        powers.append(powers[-1] * step)
    from_low = powers[nx - 1] * moment[0]
    from_high = powers[nx - 1] * moment[1]

    for copy in sends:
        copy.wait_recv()
    for s in range(1, nx):
        from_low = from_low + powers[s - 1] * moment_got[s - 1, 0]
        from_high = from_high + powers[nx - s - 1] * moment_got[s - 1, 1]
    from_low = share * from_low
    from_high = share * from_high
    for b in range(blocks):
        far_block[0, b] = block_pow[b] * from_low
        far_block[1, b] = block_pow[blocks - 1 - b] * from_high

    for copy in halos + sends:
        copy.wait_send()


def finish_kernel(nz, m, part_ref, cur_ref, head_pow, tail_pow, far_block, x_hbm, c_hbm, x, out_sem):
    blocks = m // 8
    stores = [pltpu.make_async_copy(cur_ref, c_hbm, out_sem.at[GROUPS])]
    stores[0].start()

    def finish(k, carry):
        head = head_pow[k]
        tail = tail_pow[k]
        for b in range(blocks):
            rows = slice(8 * b, 8 * b + 8)
            x[k, rows, :] = (
                part_ref[k, rows, :]
                + head * far_block[0, b, pl.ds(k, 1), :]
                + tail * far_block[1, b, pl.ds(k, 1), :]
            )
        return carry

    per = nz // GROUPS
    for part in range(GROUPS):
        each_level(part * per, (part + 1) * per, per, finish, 0)
        span = pl.ds(part * per, per)
        store = pltpu.make_async_copy(x.at[span], x_hbm.at[span], out_sem.at[part])
        store.start()
        stores.append(store)
    for store in stores:
        store.wait()


def on_device(
    initial_warmth_field,
    horizontal_motion_pair,
    z_directed_motion,
    earlier_rate_change,
    layer_depth_spacing,
    backward_spread_ratio,
    wall_warmth_bounds,
):
    nx = lax.axis_size("gx")
    ny = lax.axis_size("gy")
    nz, m, width = initial_warmth_field.shape
    assert nz == 16 and m == 128 and width == 128
    block = jax.ShapeDtypeStruct((nz, m, m), F32)
    anywhere = pl.BlockSpec(memory_space=pl.ANY)
    far_away = pl.BlockSpec(memory_space=pltpu.HBM)
    field = pltpu.VMEM((nz, m, m), F32)
    row = pltpu.VMEM((nz, m), F32)
    near = pl.BlockSpec(memory_space=pltpu.VMEM)
    carried = (
        field,
        field,
        pltpu.VMEM((nz, 8, m), F32),
        pltpu.VMEM((nz, 8, m), F32),
        pltpu.VMEM((2, m // 8, nz, m), F32),
    )
    between = pl.pallas_call(
        functools.partial(kernel, nx, ny, nz, m),
        out_shape=carried,
        in_specs=[far_away] * 7,
        out_specs=(near,) * 5,
        scratch_shapes=[
            pltpu.VMEM((nz + 2, m + 2 * OFF, m), F32),
            pltpu.VMEM((nz, m + 2 * OFF, m), F32),
            field,
            pltpu.VMEM((nz + 2, m, m), F32),
            field,
            pltpu.VMEM((nz, m, 2 * m), BF16),
            pltpu.VMEM((m // 8, nz, m), F32),
            row, row, row, row, row,
            pltpu.VMEM((2, m // 4, m), F32),
            pltpu.VMEM((2, 2, m // 4, m), F32),
            pltpu.VMEM((2, 2, nz, m), F32),
            pltpu.VMEM((2, 2, nz, m), F32),
            pltpu.VMEM((2, nz, m), F32),
            pltpu.VMEM((m // 4, m), F32),
            pltpu.VMEM((2, nz, m), F32),
            pltpu.VMEM((nx - 1, 2, nz, m), F32),
            pltpu.VMEM((2, nz, 8, m), F32),
            pltpu.SMEM((nz,), F32),
            pltpu.SMEM((nz,), F32),
            pltpu.SemaphoreType.DMA((9,)),
            pltpu.SemaphoreType.DMA((4,)),
            pltpu.SemaphoreType.DMA((4,)),
            pltpu.SemaphoreType.DMA((nx - 1,)),
            pltpu.SemaphoreType.DMA((nx - 1,)),
        ],
        compiler_params=pltpu.CompilerParams(
            collective_id=0, has_side_effects=True, vmem_limit_bytes=58 * 1024 * 1024
        ),
        cost_estimate=pl.CostEstimate(
            flops=16 * 2 * 128 * 256 * 256, bytes_accessed=8 * 1024 * 1024, transcendentals=0
        ),
    )(
        initial_warmth_field,
        horizontal_motion_pair,
        z_directed_motion,
        earlier_rate_change,
        layer_depth_spacing,
        backward_spread_ratio,
        wall_warmth_bounds,
    )
    return pl.pallas_call(
        functools.partial(finish_kernel, nz, m),
        out_shape=(block, block),
        in_specs=[near] * 5,
        out_specs=(anywhere, anywhere),
        scratch_shapes=[field, pltpu.SemaphoreType.DMA((GROUPS + 1,))],
        compiler_params=pltpu.CompilerParams(vmem_limit_bytes=16 * 1024 * 1024),
    )(*between)


def solution(mesh):
    in_specs = (
        P(None, "gx", "gy"),
        P(None, None, "gx", "gy"),
        P(None, "gx", "gy"),
        P(None, "gx", "gy"),
        P(),
        P(),
        P(None, "gx", "gy"),
    )
    out_specs = (P(None, "gx", "gy"), P(None, "gx", "gy"))
    return jax.shard_map(
        on_device, mesh=mesh, in_specs=in_specs, out_specs=out_specs, check_vma=False
    )
```

```python
import functools

import jax
import jax.numpy as jnp
from jax import lax
from jax.experimental import pallas as pl
from jax.experimental.pallas import tpu as pltpu
from jax.sharding import PartitionSpec as P

COURANT = 0.5
DIFF_Y = 0.2
DIFF_Z = 0.25
NEW_TERM_COEF = 0.75
OLD_TERM_COEF = -5.0 / 12.0

MESH = pl.DeviceIdType.MESH
F32 = jnp.float32
BF16 = jnp.bfloat16
GROUPS = 4
OFF = 8


def each_level(start, stop, step, body, carry):
    def together(i, carry):
        for j in range(step):
            carry = body(start + i * step + j, carry)
        return carry

    return lax.fori_loop(0, (stop - start) // step, together, carry)


def lanes_of(shape):
    return lax.broadcasted_iota(jnp.int32, shape, len(shape) - 1)


def rows_of(shape):
    return lax.broadcasted_iota(jnp.int32, shape, len(shape) - 2)


def kernel(
    nx, ny, nz, m,
    t_hbm, uv_hbm, w_hbm, old_hbm, dz_hbm, r_hbm, wall_hbm,
    rhs, cur, head_pow, tail_pow, far_block,
    t, u_all, v_all, w, old, green, block_pow,
    theta, scale, inv_dz, up_coef, down_coef,
    pack, pack_got, edge, edge_got, edge_fix, side_fix, moment, moment_got, shares, far, far_got, eights,
    dz_ref, r_ref,
    in_sem, halo_send, halo_recv, moment_send, moment_recv, far_send, far_recv,
):
    gx = lax.axis_index("gx")
    gy = lax.axis_index("gy")
    east, west = lax.rem(gx + 1, nx), lax.rem(gx + nx - 1, nx)
    north, south = lax.rem(gy + 1, ny), lax.rem(gy + ny - 1, ny)
    q_rows = m // 4
    blocks = m // 8
    lv = nz // nx
    inside = pl.ds(OFF, m)

    loads = [
        pltpu.make_async_copy(r_hbm, r_ref, in_sem.at[0]),
        pltpu.make_async_copy(dz_hbm, dz_ref, in_sem.at[1]),
        pltpu.make_async_copy(t_hbm, t.at[pl.ds(1, nz), inside], in_sem.at[2]),
        pltpu.make_async_copy(uv_hbm.at[1], v_all, in_sem.at[3]),
        pltpu.make_async_copy(uv_hbm.at[0], u_all.at[:, inside], in_sem.at[4]),
        pltpu.make_async_copy(wall_hbm.at[0], t.at[0, inside], in_sem.at[5]),
        pltpu.make_async_copy(wall_hbm.at[1], t.at[nz + 1, inside], in_sem.at[6]),
        pltpu.make_async_copy(w_hbm, w.at[pl.ds(1, nz)], in_sem.at[7]),
        pltpu.make_async_copy(old_hbm, old, in_sem.at[8]),
    ]
    for load in loads:
        load.start()

    barrier = pltpu.get_barrier_semaphore()
    for s in range(1, nx):
        pl.semaphore_signal(
            barrier, inc=1, device_id={"gx": lax.rem(gx + s, nx)}, device_id_type=MESH
        )
    for j in (north, south):
        pl.semaphore_signal(barrier, inc=1, device_id={"gy": j}, device_id_type=MESH)

    loads[0].wait()
    loads[1].wait()
    for k in range(nz):
        scale[k:k + 1, :] = jnp.full((1, m), r_ref[k], F32)
        inv_dz[k:k + 1, :] = 1.0 / jnp.full((1, m), dz_ref[k], F32)
    down_coef[0:1, :] = inv_dz[0:1, :]
    up_coef[nz - 1:nz, :] = inv_dz[nz - 1:nz, :]
    for k in range(nz - 1):
        between = 2.0 / jnp.full((1, m), dz_ref[k] + dz_ref[k + 1], F32)
        up_coef[k:k + 1, :] = between
        down_coef[k + 1:k + 2, :] = between
    up_coef[...] = DIFF_Z * up_coef[...] * inv_dz[...]
    down_coef[...] = DIFF_Z * down_coef[...] * inv_dz[...]
    inv_dz[...] = (-0.25 * COURANT) * inv_dz[...]
    r = scale[...]
    s = 0.5 / jnp.sqrt(r)
    theta[...] = 2.0 * jnp.log1p(s + s * s / (1.0 + jnp.sqrt(1.0 + s * s)))
    scale[...] = 1.0 / jnp.sqrt(1.0 + 4.0 * r)
    th = theta[...]
    for b in range(blocks):
        block_pow[b] = jnp.exp((-8.0 * b) * th)

    def make_tables(k, carry):
        row = rows_of((8, m))
        lane = lanes_of((8, m))
        th = theta[pl.ds(k, 1), :]
        head_pow[k] = jnp.exp(-th * row.astype(F32))
        tail_pow[k] = jnp.exp(-th * (7 - row).astype(F32))
        return carry

    each_level(0, nz, 4, make_tables, 0)

    for load in loads[2:5]:
        load.wait()

    def make_pack(k, carry):
        pt, pv = carry
        pair = lanes_of((q_rows, m)) // 2
        for h in range(4):
            turn = 32 * h + 2 * k + 1
            mine = pair == 16 * h + k
            here = t[k + 1, OFF + h * q_rows:OFF + (h + 1) * q_rows, :]
            pt = jnp.where(mine, pltpu.roll(here, turn, 1), pt)
            pv = jnp.where(
                mine, pltpu.roll(v_all[k, h * q_rows:(h + 1) * q_rows, :], turn, 1), pv
            )
        edge[0, 0, pl.ds(k, 1), :] = t[k + 1, OFF + m - 1:OFF + m, :]
        edge[0, 1, pl.ds(k, 1), :] = u_all[k, OFF + m - 1:OFF + m, :]
        edge[1, 0, pl.ds(k, 1), :] = t[k + 1, OFF:OFF + 1, :]
        edge[1, 1, pl.ds(k, 1), :] = u_all[k, OFF:OFF + 1, :]
        return pt, pv

    blank = jnp.zeros((q_rows, m), F32)
    pt, pv = each_level(0, nz, 4, make_pack, (blank, blank))
    pack[0] = pt
    pack[1] = pv

    pl.semaphore_wait(barrier, nx + 1)

    def halo(src, dst, i, where):
        copy = pltpu.make_async_remote_copy(
            src_ref=src, dst_ref=dst, send_sem=halo_send.at[i], recv_sem=halo_recv.at[i],
            device_id=where, device_id_type=MESH,
        )
        copy.start()
        return copy

    halos = [
        halo(pack, pack_got.at[0], 0, {"gy": north}),
        halo(pack, pack_got.at[1], 1, {"gy": south}),
        halo(edge.at[0], edge_got.at[0], 2, {"gx": east}),
        halo(edge.at[1], edge_got.at[1], 3, {"gx": west}),
    ]

    for load in loads[5:]:
        load.wait()
    w[0] = -w[1]
    w[nz + 1] = -w[nz]

    def inner(k, carry):
        row = rows_of((q_rows, m))
        lane = lanes_of((q_rows, m))
        one = pl.ds(k, 1)
        up, down, idz = up_coef[one, :], down_coef[one, :], inv_dz[one, :]
        low_sum = jnp.zeros((8, m), F32)
        high_sum = jnp.zeros((8, m), F32)
        for h in range(4):
            rows = slice(h * q_rows, (h + 1) * q_rows)
            pad = slice(OFF + h * q_rows, OFF + (h + 1) * q_rows)
            after = slice(OFF + h * q_rows + 1, OFF + (h + 1) * q_rows + 1)
            before = slice(OFF + h * q_rows - 1, OFF + (h + 1) * q_rows - 1)
            here = t[k + 1, pad, :]
            u = u_all[k, pad, :]
            v = v_all[k, rows, :]
            fx = (u + u_all[k, after, :]) * (here + t[k + 1, after, :])
            gx_flux = (u_all[k, before, :] + u) * (t[k + 1, before, :] + here)
            if h == 3:
                fx = jnp.where(row == q_rows - 1, 0.0, fx)
            if h == 0:
                gx_flux = jnp.where(row == 0, 0.0, gx_flux)
            right = pltpu.roll(here, m - 1, 1)
            fy = (v + pltpu.roll(v, m - 1, 1)) * (here + right)
            fy = jnp.where(lane == m - 1, 0.0, fy)
            div = (fx - gx_flux) + (fy - pltpu.roll(fy, 1, 1))
            lap = jnp.where(lane == m - 1, 0.0, right) + jnp.where(
                lane == 0, 0.0, pltpu.roll(here, 1, 1)
            )
            below, above = t[k, pad, :], t[k + 2, pad, :]
            wk = w[k + 1, rows, :]
            fz = (wk + w[k + 2, rows, :]) * (here + above) - (w[k, rows, :] + wk) * (below + here)
            value = (
                (-0.25 * COURANT) * div
                + idz * fz
                + DIFF_Y * (lap - 2.0 * here)
                + (up * (above - here) - down * (here - below))
            )
            b = here + NEW_TERM_COEF * value + OLD_TERM_COEF * old[k, rows, :]
            cur[k, rows, :] = value
            rhs[k, rows, :] = b
            for i in range(4):
                c = 4 * h + i
                part = b[8 * i:8 * i + 8, :]
                low_sum = low_sum + block_pow[blocks - 1 - c, one, :] * part
                high_sum = high_sum + block_pow[c, one, :] * part
        eights[0, k] = tail_pow[k] * low_sum
        eights[1, k] = head_pow[k] * high_sum
        return carry

    each_level(0, nz, 4, inner, 0)

    lane1 = lanes_of((1, m))
    th_lane = jnp.zeros((1, m), F32)
    for k in range(nz):
        th_lane = jnp.where(lax.rem(lane1, 32) // 2 == k, theta[k:k + 1, :], th_lane)
    cell = rows_of((q_rows, m)) + (lanes_of((q_rows, m)) // 32) * q_rows
    weight_f = NEW_TERM_COEF * jnp.exp(-th_lane * cell.astype(F32))
    weight_g = NEW_TERM_COEF * jnp.exp(-th_lane * (m - 1 - cell).astype(F32))
    q_end = jnp.exp(-(m - 1.0) * th)
    sums_low = jnp.sum(eights[0], axis=1)
    sums_high = jnp.sum(eights[1], axis=1)

    for copy in halos:
        copy.wait_recv()

    first = lax.rem(lanes_of((q_rows, m)), 2) == 1
    near_t = jnp.where(
        first, pltpu.roll(pack_got[0, 0], 1, 1), pltpu.roll(pack_got[1, 0], m - 1, 1)
    )
    near_v = jnp.where(
        first, pltpu.roll(pack_got[0, 1], 1, 1), pltpu.roll(pack_got[1, 1], m - 1, 1)
    )
    flux = (pack[1] + near_v) * (pack[0] + near_t)
    fix = DIFF_Y * near_t + jnp.where(first, 0.25 * COURANT, -0.25 * COURANT) * flux
    side_fix[...] = fix
    low = (0.25 * COURANT) * (edge_got[0, 1] + edge[1, 1]) * (edge_got[0, 0] + edge[1, 0])
    top = (-0.25 * COURANT) * (edge_got[1, 1] + edge[0, 1]) * (edge_got[1, 0] + edge[0, 0])
    edge_fix[0] = low
    edge_fix[1] = top

    level = rows_of((nz, m))
    lane = lanes_of((nz, m))

    def spread(weights):
        line = jnp.sum(weights * fix, axis=0, keepdims=True)
        line = line + pltpu.roll(line, 32, 1)
        line = line + pltpu.roll(line, 64, 1)
        wide = jnp.broadcast_to(line, (nz, m))
        last = jnp.sum(jnp.where(lane == 2 * level, wide, 0.0), axis=1, keepdims=True)
        head = jnp.sum(jnp.where(lane == 2 * level + 1, wide, 0.0), axis=1, keepdims=True)
        return jnp.where(lane == 0, head, 0.0) + jnp.where(lane == m - 1, last, 0.0)

    own_low = sums_low + NEW_TERM_COEF * (q_end * low + top) + spread(weight_g)
    own_high = sums_high + NEW_TERM_COEF * (low + q_end * top) + spread(weight_f)
    for q in range(nx):
        moment[q, 0:lv, :] = own_low[q * lv:(q + 1) * lv, :]
        moment[q, lv:2 * lv, :] = own_high[q * lv:(q + 1) * lv, :]

    sends = []
    for s in range(1, nx):
        there = lax.rem(gx + s, nx)
        copy = pltpu.make_async_remote_copy(
            src_ref=moment.at[there], dst_ref=moment_got.at[s],
            send_sem=moment_send.at[s], recv_sem=moment_recv.at[s],
            device_id={"gx": there}, device_id_type=MESH,
        )
        copy.start()
        sends.append(copy)

    step = jnp.exp(-float(m) * th)
    share = scale[...] * jnp.exp(-th) / (1.0 - jnp.exp(-float(m * nx) * th))
    for q in range(nx):
        shares[q, 0:lv, :] = share[q * lv:(q + 1) * lv, :]
        shares[q, lv:2 * lv, :] = step[q * lv:(q + 1) * lv, :]

    def local_inverse(k, carry):
        row8 = rows_of((8, m))
        lane8 = lanes_of((8, m))
        th = theta[pl.ds(k, 1), :]
        level_scale = scale[pl.ds(k, 1), :]
        near = level_scale * jnp.exp(-th * jnp.abs(row8 - lane8).astype(F32))
        wrap = level_scale * jnp.exp(-th * (row8 - lane8 + m).astype(F32))
        for b0 in range(0, blocks, 2):
            full = jnp.concatenate(
                [
                    pltpu.roll(jnp.where(lane8 < m - 8 * c, near, wrap), 8 * c, 1)
                    if c
                    else near
                    for c in (b0, b0 + 1)
                ],
                axis=0,
            )
            high = full.astype(BF16)
            green[k, 8 * b0:8 * b0 + 16, 0:m] = high
            green[k, 8 * b0:8 * b0 + 16, m:2 * m] = (full - high.astype(F32)).astype(BF16)
        return carry

    each_level(0, nz, 4, local_inverse, 0)

    for copy in sends:
        copy.wait_recv()
    mine = shares[gx]
    powers = [mine[0:lv, :]]
    for s in range(1, nx):
        powers.append(powers[-1] * mine[lv:2 * lv, :])
    lows = [moment[gx, 0:lv, :]] + [moment_got[s, 0:lv, :] for s in range(1, nx)]
    highs = [moment[gx, lv:2 * lv, :]] + [moment_got[s, lv:2 * lv, :] for s in range(1, nx)]
    returns = []
    for e in range(nx):
        from_low = jnp.zeros((lv, m), F32)
        from_high = jnp.zeros((lv, m), F32)
        for s in range(1, nx + 1):
            from_low = from_low + powers[s - 1] * lows[(s - e) % nx]
            from_high = from_high + powers[s - 1] * highs[(-s - e) % nx]
        far[e, 0:lv, :] = from_low
        far[e, lv:2 * lv, :] = from_high
        if e:
            copy = pltpu.make_async_remote_copy(
                src_ref=far.at[e], dst_ref=far_got.at[gx],
                send_sem=far_send.at[e], recv_sem=far_recv.at[e],
                device_id={"gx": lax.rem(gx + e, nx)}, device_id_type=MESH,
            )
            copy.start()
            returns.append(copy)
    far_got[gx] = far[0]

    def local_solve(k, carry):
        lane = lanes_of((q_rows, m))
        row = rows_of((q_rows, m))
        side = (lane == 0) | (lane == m - 1)
        parts = []
        for h in range(4):
            rows = slice(h * q_rows, (h + 1) * q_rows)
            extra = jnp.where(
                side, pltpu.roll(side_fix[...], m - 1 - 32 * h - 2 * k, 1), 0.0
            )
            if h == 0:
                extra = extra + jnp.where(row == 0, edge_fix[0, pl.ds(k, 1), :], 0.0)
            if h == 3:
                extra = extra + jnp.where(row == q_rows - 1, edge_fix[1, pl.ds(k, 1), :], 0.0)
            cur[k, rows, :] = cur[k, rows, :] + extra
            parts.append(rhs[k, rows, :] + NEW_TERM_COEF * extra)
        b = jnp.concatenate(parts, axis=0)
        high = b.astype(BF16)
        pair = jnp.concatenate([high, (b - high.astype(F32)).astype(BF16)], axis=1)
        both = jnp.dot(
            green[k], jnp.concatenate([pair, pair], axis=0), preferred_element_type=F32
        )
        rhs[k] = both[:, 0:m] + both[:, m:2 * m]
        return carry

    each_level(0, nz, 4, local_solve, 0)

    for copy in returns:
        copy.wait_recv()
    from_low = jnp.concatenate([far_got[q, 0:lv, :] for q in range(nx)], axis=0)
    from_high = jnp.concatenate([far_got[q, lv:2 * lv, :] for q in range(nx)], axis=0)
    for b in range(blocks):
        far_block[0, b] = block_pow[b] * from_low
        far_block[1, b] = block_pow[blocks - 1 - b] * from_high

    for copy in halos + sends + returns:
        copy.wait_send()


def finish_kernel(nz, m, part_ref, cur_ref, head_pow, tail_pow, far_block, x_hbm, c_hbm, x, out_sem):
    blocks = m // 8
    stores = [pltpu.make_async_copy(cur_ref, c_hbm, out_sem.at[GROUPS])]
    stores[0].start()

    def finish(k, carry):
        head = head_pow[k]
        tail = tail_pow[k]
        for b in range(blocks):
            rows = slice(8 * b, 8 * b + 8)
            x[k, rows, :] = (
                part_ref[k, rows, :]
                + head * far_block[0, b, pl.ds(k, 1), :]
                + tail * far_block[1, b, pl.ds(k, 1), :]
            )
        return carry

    per = nz // GROUPS
    for part in range(GROUPS):
        each_level(part * per, (part + 1) * per, per, finish, 0)
        span = pl.ds(part * per, per)
        store = pltpu.make_async_copy(x.at[span], x_hbm.at[span], out_sem.at[part])
        store.start()
        stores.append(store)
    for store in stores:
        store.wait()


def on_device(
    initial_warmth_field,
    horizontal_motion_pair,
    z_directed_motion,
    earlier_rate_change,
    layer_depth_spacing,
    backward_spread_ratio,
    wall_warmth_bounds,
):
    nx = lax.axis_size("gx")
    ny = lax.axis_size("gy")
    nz, m, width = initial_warmth_field.shape
    assert nz == 16 and m == 128 and width == 128
    block = jax.ShapeDtypeStruct((nz, m, m), F32)
    anywhere = pl.BlockSpec(memory_space=pl.ANY)
    far_away = pl.BlockSpec(memory_space=pltpu.HBM)
    field = pltpu.VMEM((nz, m, m), F32)
    row = pltpu.VMEM((nz, m), F32)
    by_owner = pltpu.VMEM((nx, 2 * (nz // nx), m), F32)
    each_peer = pltpu.SemaphoreType.DMA((nx,))
    near = pl.BlockSpec(memory_space=pltpu.VMEM)
    carried = (
        field,
        field,
        pltpu.VMEM((nz, 8, m), F32),
        pltpu.VMEM((nz, 8, m), F32),
        pltpu.VMEM((2, m // 8, nz, m), F32),
    )
    between = pl.pallas_call(
        functools.partial(kernel, nx, ny, nz, m),
        out_shape=carried,
        in_specs=[far_away] * 7,
        out_specs=(near,) * 5,
        scratch_shapes=[
            pltpu.VMEM((nz + 2, m + 2 * OFF, m), F32),
            pltpu.VMEM((nz, m + 2 * OFF, m), F32),
            field,
            pltpu.VMEM((nz + 2, m, m), F32),
            field,
            pltpu.VMEM((nz, m, 2 * m), BF16),
            pltpu.VMEM((m // 8, nz, m), F32),
            row, row, row, row, row,
            pltpu.VMEM((2, m // 4, m), F32),
            pltpu.VMEM((2, 2, m // 4, m), F32),
            pltpu.VMEM((2, 2, nz, m), F32),
            pltpu.VMEM((2, 2, nz, m), F32),
            pltpu.VMEM((2, nz, m), F32),
            pltpu.VMEM((m // 4, m), F32),
            by_owner, by_owner, by_owner, by_owner, by_owner,
            pltpu.VMEM((2, nz, 8, m), F32),
            pltpu.SMEM((nz,), F32),
            pltpu.SMEM((nz,), F32),
            pltpu.SemaphoreType.DMA((9,)),
            pltpu.SemaphoreType.DMA((4,)),
            pltpu.SemaphoreType.DMA((4,)),
            each_peer, each_peer, each_peer, each_peer,
        ],
        compiler_params=pltpu.CompilerParams(
            collective_id=0, has_side_effects=True, vmem_limit_bytes=58 * 1024 * 1024
        ),
        cost_estimate=pl.CostEstimate(
            flops=16 * 2 * 128 * 256 * 256, bytes_accessed=8 * 1024 * 1024, transcendentals=0
        ),
    )(
        initial_warmth_field,
        horizontal_motion_pair,
        z_directed_motion,
        earlier_rate_change,
        layer_depth_spacing,
        backward_spread_ratio,
        wall_warmth_bounds,
    )
    return pl.pallas_call(
        functools.partial(finish_kernel, nz, m),
        out_shape=(block, block),
        in_specs=[near] * 5,
        out_specs=(anywhere, anywhere),
        scratch_shapes=[field, pltpu.SemaphoreType.DMA((GROUPS + 1,))],
        compiler_params=pltpu.CompilerParams(vmem_limit_bytes=16 * 1024 * 1024),
    )(*between)


def solution(mesh):
    in_specs = (
        P(None, "gx", "gy"),
        P(None, None, "gx", "gy"),
        P(None, "gx", "gy"),
        P(None, "gx", "gy"),
        P(),
        P(),
        P(None, "gx", "gy"),
    )
    out_specs = (P(None, "gx", "gy"), P(None, "gx", "gy"))
    return jax.shard_map(
        on_device, mesh=mesh, in_specs=in_specs, out_specs=out_specs, check_vma=False
    )
```

```python
import functools

import jax
import jax.numpy as jnp
from jax import lax
from jax.experimental import pallas as pl
from jax.experimental.pallas import tpu as pltpu
from jax.sharding import PartitionSpec as P

COURANT = 0.5
DIFF_Y = 0.2
DIFF_Z = 0.25
NEW_TERM_COEF = 0.75
OLD_TERM_COEF = -5.0 / 12.0

MESH = pl.DeviceIdType.MESH
F32 = jnp.float32
BF16 = jnp.bfloat16
GROUPS = 4
OFF = 8


def each_level(start, stop, step, body, carry):
    def together(i, carry):
        for j in range(step):
            carry = body(start + i * step + j, carry)
        return carry

    return lax.fori_loop(0, (stop - start) // step, together, carry)


def lanes_of(shape):
    return lax.broadcasted_iota(jnp.int32, shape, len(shape) - 1)


def rows_of(shape):
    return lax.broadcasted_iota(jnp.int32, shape, len(shape) - 2)


def kernel(
    nx, ny, nz, m,
    t_hbm, uv_hbm, w_hbm, old_hbm, dz_hbm, r_hbm, wall_hbm,
    rhs, cur, head_pow, tail_pow, far_block,
    t, u_all, v_all, w, old, green, block_pow,
    theta, scale, inv_dz, up_coef, down_coef,
    pack, pack_got, edge, edge_got, edge_fix, side_fix, moment, moment_got, eights,
    dz_ref, r_ref,
    in_sem, halo_send, halo_recv, moment_send, moment_recv,
):
    gx = lax.axis_index("gx")
    gy = lax.axis_index("gy")
    east, west = lax.rem(gx + 1, nx), lax.rem(gx + nx - 1, nx)
    north, south = lax.rem(gy + 1, ny), lax.rem(gy + ny - 1, ny)
    q_rows = m // 4
    blocks = m // 8
    inside = pl.ds(OFF, m)

    loads = [
        pltpu.make_async_copy(r_hbm, r_ref, in_sem.at[0]),
        pltpu.make_async_copy(dz_hbm, dz_ref, in_sem.at[1]),
        pltpu.make_async_copy(t_hbm, t.at[pl.ds(1, nz), inside], in_sem.at[2]),
        pltpu.make_async_copy(uv_hbm.at[1], v_all, in_sem.at[3]),
        pltpu.make_async_copy(uv_hbm.at[0], u_all.at[:, inside], in_sem.at[4]),
        pltpu.make_async_copy(wall_hbm.at[0], t.at[0, inside], in_sem.at[5]),
        pltpu.make_async_copy(wall_hbm.at[1], t.at[nz + 1, inside], in_sem.at[6]),
        pltpu.make_async_copy(w_hbm, w.at[pl.ds(1, nz)], in_sem.at[7]),
        pltpu.make_async_copy(old_hbm, old, in_sem.at[8]),
    ]
    for load in loads[:4]:
        load.start()

    barrier = pltpu.get_barrier_semaphore()
    for s in range(1, nx):
        pl.semaphore_signal(
            barrier, inc=1, device_id={"gx": lax.rem(gx + s, nx)}, device_id_type=MESH
        )
    for j in (north, south):
        pl.semaphore_signal(barrier, inc=1, device_id={"gy": j}, device_id_type=MESH)

    for load in loads[4:]:
        load.start()

    loads[0].wait()
    loads[1].wait()
    for k in range(nz):
        scale[k:k + 1, :] = jnp.full((1, m), r_ref[k], F32)
        inv_dz[k:k + 1, :] = 1.0 / jnp.full((1, m), dz_ref[k], F32)
    down_coef[0:1, :] = inv_dz[0:1, :]
    up_coef[nz - 1:nz, :] = inv_dz[nz - 1:nz, :]
    for k in range(nz - 1):
        between = 2.0 / jnp.full((1, m), dz_ref[k] + dz_ref[k + 1], F32)
        up_coef[k:k + 1, :] = between
        down_coef[k + 1:k + 2, :] = between
    up_coef[...] = DIFF_Z * up_coef[...] * inv_dz[...]
    down_coef[...] = DIFF_Z * down_coef[...] * inv_dz[...]
    inv_dz[...] = (-0.25 * COURANT) * inv_dz[...]
    r = scale[...]
    s = 0.5 / jnp.sqrt(r)
    theta[...] = 2.0 * jnp.log1p(s + s * s / (1.0 + jnp.sqrt(1.0 + s * s)))
    scale[...] = 1.0 / jnp.sqrt(1.0 + 4.0 * r)
    th = theta[...]
    for b in range(blocks):
        block_pow[b] = jnp.exp((-8.0 * b) * th)

    def make_tables(k, carry):
        row = rows_of((8, m))
        lane = lanes_of((8, m))
        th = theta[pl.ds(k, 1), :]
        head_pow[k] = jnp.exp(-th * row.astype(F32))
        tail_pow[k] = jnp.exp(-th * (7 - row).astype(F32))
        return carry

    each_level(0, nz, 4, make_tables, 0)

    for load in loads[2:5]:
        load.wait()

    def make_pack(k, carry):
        pt, pv = carry
        pair = lanes_of((q_rows, m)) // 2
        for h in range(4):
            turn = 32 * h + 2 * k + 1
            mine = pair == 16 * h + k
            here = t[k + 1, OFF + h * q_rows:OFF + (h + 1) * q_rows, :]
            pt = jnp.where(mine, pltpu.roll(here, turn, 1), pt)
            pv = jnp.where(
                mine, pltpu.roll(v_all[k, h * q_rows:(h + 1) * q_rows, :], turn, 1), pv
            )
        edge[0, 0, pl.ds(k, 1), :] = t[k + 1, OFF + m - 1:OFF + m, :]
        edge[0, 1, pl.ds(k, 1), :] = u_all[k, OFF + m - 1:OFF + m, :]
        edge[1, 0, pl.ds(k, 1), :] = t[k + 1, OFF:OFF + 1, :]
        edge[1, 1, pl.ds(k, 1), :] = u_all[k, OFF:OFF + 1, :]
        return pt, pv

    blank = jnp.zeros((q_rows, m), F32)
    pt, pv = each_level(0, nz, 4, make_pack, (blank, blank))
    pack[0] = pt
    pack[1] = pv

    pl.semaphore_wait(barrier, nx + 1)

    def halo(src, dst, i, where):
        copy = pltpu.make_async_remote_copy(
            src_ref=src, dst_ref=dst, send_sem=halo_send.at[i], recv_sem=halo_recv.at[i],
            device_id=where, device_id_type=MESH,
        )
        copy.start()
        return copy

    halos = [
        halo(pack, pack_got.at[0], 0, {"gy": north}),
        halo(pack, pack_got.at[1], 1, {"gy": south}),
        halo(edge.at[0], edge_got.at[0], 2, {"gx": east}),
        halo(edge.at[1], edge_got.at[1], 3, {"gx": west}),
    ]

    for load in loads[5:]:
        load.wait()
    w[0] = -w[1]
    w[nz + 1] = -w[nz]

    def inner(k, carry):
        row = rows_of((q_rows, m))
        lane = lanes_of((q_rows, m))
        one = pl.ds(k, 1)
        up, down, idz = up_coef[one, :], down_coef[one, :], inv_dz[one, :]
        low_sum = jnp.zeros((8, m), F32)
        high_sum = jnp.zeros((8, m), F32)
        for h in range(4):
            rows = slice(h * q_rows, (h + 1) * q_rows)
            pad = slice(OFF + h * q_rows, OFF + (h + 1) * q_rows)
            after = slice(OFF + h * q_rows + 1, OFF + (h + 1) * q_rows + 1)
            before = slice(OFF + h * q_rows - 1, OFF + (h + 1) * q_rows - 1)
            here = t[k + 1, pad, :]
            u = u_all[k, pad, :]
            v = v_all[k, rows, :]
            fx = (u + u_all[k, after, :]) * (here + t[k + 1, after, :])
            gx_flux = (u_all[k, before, :] + u) * (t[k + 1, before, :] + here)
            if h == 3:
                fx = jnp.where(row == q_rows - 1, 0.0, fx)
            if h == 0:
                gx_flux = jnp.where(row == 0, 0.0, gx_flux)
            right = pltpu.roll(here, m - 1, 1)
            fy = (v + pltpu.roll(v, m - 1, 1)) * (here + right)
            fy = jnp.where(lane == m - 1, 0.0, fy)
            div = (fx - gx_flux) + (fy - pltpu.roll(fy, 1, 1))
            lap = jnp.where(lane == m - 1, 0.0, right) + jnp.where(
                lane == 0, 0.0, pltpu.roll(here, 1, 1)
            )
            below, above = t[k, pad, :], t[k + 2, pad, :]
            wk = w[k + 1, rows, :]
            fz = (wk + w[k + 2, rows, :]) * (here + above) - (w[k, rows, :] + wk) * (below + here)
            value = (
                (-0.25 * COURANT) * div
                + idz * fz
                + DIFF_Y * (lap - 2.0 * here)
                + (up * (above - here) - down * (here - below))
            )
            b = here + NEW_TERM_COEF * value + OLD_TERM_COEF * old[k, rows, :]
            cur[k, rows, :] = value
            rhs[k, rows, :] = b
            for i in range(4):
                c = 4 * h + i
                part = b[8 * i:8 * i + 8, :]
                low_sum = low_sum + block_pow[blocks - 1 - c, one, :] * part
                high_sum = high_sum + block_pow[c, one, :] * part
        eights[0, k] = tail_pow[k] * low_sum
        eights[1, k] = head_pow[k] * high_sum
        return carry

    each_level(0, nz, 4, inner, 0)

    lane1 = lanes_of((1, m))
    th_lane = jnp.zeros((1, m), F32)
    for k in range(nz):
        th_lane = jnp.where(lax.rem(lane1, 32) // 2 == k, theta[k:k + 1, :], th_lane)
    cell = rows_of((q_rows, m)) + (lanes_of((q_rows, m)) // 32) * q_rows
    weight_f = NEW_TERM_COEF * jnp.exp(-th_lane * cell.astype(F32))
    weight_g = NEW_TERM_COEF * jnp.exp(-th_lane * (m - 1 - cell).astype(F32))
    q_end = jnp.exp(-(m - 1.0) * th)
    sums_low = jnp.sum(eights[0], axis=1)
    sums_high = jnp.sum(eights[1], axis=1)

    for copy in halos:
        copy.wait_recv()

    first = lax.rem(lanes_of((q_rows, m)), 2) == 1
    near_t = jnp.where(
        first, pltpu.roll(pack_got[0, 0], 1, 1), pltpu.roll(pack_got[1, 0], m - 1, 1)
    )
    near_v = jnp.where(
        first, pltpu.roll(pack_got[0, 1], 1, 1), pltpu.roll(pack_got[1, 1], m - 1, 1)
    )
    flux = (pack[1] + near_v) * (pack[0] + near_t)
    fix = DIFF_Y * near_t + jnp.where(first, 0.25 * COURANT, -0.25 * COURANT) * flux
    side_fix[...] = fix
    low = (0.25 * COURANT) * (edge_got[0, 1] + edge[1, 1]) * (edge_got[0, 0] + edge[1, 0])
    top = (-0.25 * COURANT) * (edge_got[1, 1] + edge[0, 1]) * (edge_got[1, 0] + edge[0, 0])
    edge_fix[0] = low
    edge_fix[1] = top

    level = rows_of((nz, m))
    lane = lanes_of((nz, m))

    def spread(weights):
        line = jnp.sum(weights * fix, axis=0, keepdims=True)
        line = line + pltpu.roll(line, 32, 1)
        line = line + pltpu.roll(line, 64, 1)
        wide = jnp.broadcast_to(line, (nz, m))
        last = jnp.sum(jnp.where(lane == 2 * level, wide, 0.0), axis=1, keepdims=True)
        head = jnp.sum(jnp.where(lane == 2 * level + 1, wide, 0.0), axis=1, keepdims=True)
        return jnp.where(lane == 0, head, 0.0) + jnp.where(lane == m - 1, last, 0.0)

    moment[0] = sums_low + NEW_TERM_COEF * (q_end * low + top) + spread(weight_g)
    moment[1] = sums_high + NEW_TERM_COEF * (low + q_end * top) + spread(weight_f)

    sends = [
        pltpu.make_async_remote_copy(
            src_ref=moment, dst_ref=moment_got.at[s - 1],
            send_sem=moment_send.at[s - 1], recv_sem=moment_recv.at[s - 1],
            device_id={"gx": lax.rem(gx + s, nx)}, device_id_type=MESH,
        )
        for s in sorted(range(1, nx), key=lambda s: abs(2 * s - nx))
    ]
    for copy in sends:
        copy.start()

    def local_inverse(k, carry):
        row8 = rows_of((8, m))
        lane8 = lanes_of((8, m))
        th = theta[pl.ds(k, 1), :]
        level_scale = scale[pl.ds(k, 1), :]
        near = level_scale * jnp.exp(-th * jnp.abs(row8 - lane8).astype(F32))
        wrap = level_scale * jnp.exp(-th * (row8 - lane8 + m).astype(F32))
        for b0 in range(0, blocks, 2):
            full = jnp.concatenate(
                [
                    pltpu.roll(jnp.where(lane8 < m - 8 * c, near, wrap), 8 * c, 1)
                    if c
                    else near
                    for c in (b0, b0 + 1)
                ],
                axis=0,
            )
            high = full.astype(BF16)
            green[k, 8 * b0:8 * b0 + 16, 0:m] = high
            green[k, 8 * b0:8 * b0 + 16, m:2 * m] = (full - high.astype(F32)).astype(BF16)
        return carry

    each_level(0, nz, 4, local_inverse, 0)

    def local_solve(k, carry):
        lane = lanes_of((q_rows, m))
        row = rows_of((q_rows, m))
        side = (lane == 0) | (lane == m - 1)
        parts = []
        for h in range(4):
            rows = slice(h * q_rows, (h + 1) * q_rows)
            extra = jnp.where(
                side, pltpu.roll(side_fix[...], m - 1 - 32 * h - 2 * k, 1), 0.0
            )
            if h == 0:
                extra = extra + jnp.where(row == 0, edge_fix[0, pl.ds(k, 1), :], 0.0)
            if h == 3:
                extra = extra + jnp.where(row == q_rows - 1, edge_fix[1, pl.ds(k, 1), :], 0.0)
            cur[k, rows, :] = cur[k, rows, :] + extra
            parts.append(rhs[k, rows, :] + NEW_TERM_COEF * extra)
        b = jnp.concatenate(parts, axis=0)
        high = b.astype(BF16)
        pair = jnp.concatenate([high, (b - high.astype(F32)).astype(BF16)], axis=1)
        both = jnp.dot(
            green[k], jnp.concatenate([pair, pair], axis=0), preferred_element_type=F32
        )
        rhs[k] = both[:, 0:m] + both[:, m:2 * m]
        return carry

    each_level(0, nz, 4, local_solve, 0)

    step = jnp.exp(-float(m) * th)
    share = scale[...] * jnp.exp(-th) / (1.0 - jnp.exp(-float(m * nx) * th))
    powers = [jnp.ones_like(step)]
    for s in range(1, nx):
        powers.append(powers[-1] * step)
    from_low = powers[nx - 1] * moment[0]
    from_high = powers[nx - 1] * moment[1]

    for copy in sends:
        copy.wait_recv()
    for s in range(1, nx):
        from_low = from_low + powers[s - 1] * moment_got[s - 1, 0]
        from_high = from_high + powers[nx - s - 1] * moment_got[s - 1, 1]
    from_low = share * from_low
    from_high = share * from_high
    for b in range(blocks):
        far_block[0, b] = block_pow[b] * from_low
        far_block[1, b] = block_pow[blocks - 1 - b] * from_high

    for copy in halos + sends:
        copy.wait_send()


def finish_kernel(nz, m, part_ref, cur_ref, head_pow, tail_pow, far_block, x_hbm, c_hbm, x, out_sem):
    blocks = m // 8
    stores = [pltpu.make_async_copy(cur_ref, c_hbm, out_sem.at[GROUPS])]
    stores[0].start()

    def finish(k, carry):
        head = head_pow[k]
        tail = tail_pow[k]
        for b in range(blocks):
            rows = slice(8 * b, 8 * b + 8)
            x[k, rows, :] = (
                part_ref[k, rows, :]
                + head * far_block[0, b, pl.ds(k, 1), :]
                + tail * far_block[1, b, pl.ds(k, 1), :]
            )
        return carry

    per = nz // GROUPS
    for part in range(GROUPS):
        each_level(part * per, (part + 1) * per, per, finish, 0)
        span = pl.ds(part * per, per)
        store = pltpu.make_async_copy(x.at[span], x_hbm.at[span], out_sem.at[part])
        store.start()
        stores.append(store)
    for store in stores:
        store.wait()


def on_device(
    initial_warmth_field,
    horizontal_motion_pair,
    z_directed_motion,
    earlier_rate_change,
    layer_depth_spacing,
    backward_spread_ratio,
    wall_warmth_bounds,
):
    nx = lax.axis_size("gx")
    ny = lax.axis_size("gy")
    nz, m, width = initial_warmth_field.shape
    assert nz == 16 and m == 128 and width == 128
    block = jax.ShapeDtypeStruct((nz, m, m), F32)
    anywhere = pl.BlockSpec(memory_space=pl.ANY)
    far_away = pl.BlockSpec(memory_space=pltpu.HBM)
    field = pltpu.VMEM((nz, m, m), F32)
    row = pltpu.VMEM((nz, m), F32)
    near = pl.BlockSpec(memory_space=pltpu.VMEM)
    carried = (
        field,
        field,
        pltpu.VMEM((nz, 8, m), F32),
        pltpu.VMEM((nz, 8, m), F32),
        pltpu.VMEM((2, m // 8, nz, m), F32),
    )
    between = pl.pallas_call(
        functools.partial(kernel, nx, ny, nz, m),
        out_shape=carried,
        in_specs=[far_away] * 7,
        out_specs=(near,) * 5,
        scratch_shapes=[
            pltpu.VMEM((nz + 2, m + 2 * OFF, m), F32),
            pltpu.VMEM((nz, m + 2 * OFF, m), F32),
            field,
            pltpu.VMEM((nz + 2, m, m), F32),
            field,
            pltpu.VMEM((nz, m, 2 * m), BF16),
            pltpu.VMEM((m // 8, nz, m), F32),
            row, row, row, row, row,
            pltpu.VMEM((2, m // 4, m), F32),
            pltpu.VMEM((2, 2, m // 4, m), F32),
            pltpu.VMEM((2, 2, nz, m), F32),
            pltpu.VMEM((2, 2, nz, m), F32),
            pltpu.VMEM((2, nz, m), F32),
            pltpu.VMEM((m // 4, m), F32),
            pltpu.VMEM((2, nz, m), F32),
            pltpu.VMEM((nx - 1, 2, nz, m), F32),
            pltpu.VMEM((2, nz, 8, m), F32),
            pltpu.SMEM((nz,), F32),
            pltpu.SMEM((nz,), F32),
            pltpu.SemaphoreType.DMA((9,)),
            pltpu.SemaphoreType.DMA((4,)),
            pltpu.SemaphoreType.DMA((4,)),
            pltpu.SemaphoreType.DMA((nx - 1,)),
            pltpu.SemaphoreType.DMA((nx - 1,)),
        ],
        compiler_params=pltpu.CompilerParams(
            collective_id=0, has_side_effects=True, vmem_limit_bytes=58 * 1024 * 1024
        ),
        cost_estimate=pl.CostEstimate(
            flops=16 * 2 * 128 * 256 * 256, bytes_accessed=8 * 1024 * 1024, transcendentals=0
        ),
    )(
        initial_warmth_field,
        horizontal_motion_pair,
        z_directed_motion,
        earlier_rate_change,
        layer_depth_spacing,
        backward_spread_ratio,
        wall_warmth_bounds,
    )
    return pl.pallas_call(
        functools.partial(finish_kernel, nz, m),
        out_shape=(block, block),
        in_specs=[near] * 5,
        out_specs=(anywhere, anywhere),
        scratch_shapes=[field, pltpu.SemaphoreType.DMA((GROUPS + 1,))],
        compiler_params=pltpu.CompilerParams(vmem_limit_bytes=16 * 1024 * 1024),
    )(*between)


def solution(mesh):
    in_specs = (
        P(None, "gx", "gy"),
        P(None, None, "gx", "gy"),
        P(None, "gx", "gy"),
        P(None, "gx", "gy"),
        P(),
        P(),
        P(None, "gx", "gy"),
    )
    out_specs = (P(None, "gx", "gy"), P(None, "gx", "gy"))
    return jax.shard_map(
        on_device, mesh=mesh, in_specs=in_specs, out_specs=out_specs, check_vma=False
    )
```

```python
import functools

import jax
import jax.numpy as jnp
from jax import lax
from jax.experimental import pallas as pl
from jax.experimental.pallas import tpu as pltpu
from jax.sharding import PartitionSpec as P

COURANT = 0.5
DIFF_Y = 0.2
DIFF_Z = 0.25
NEW_TERM_COEF = 0.75
OLD_TERM_COEF = -5.0 / 12.0

MESH = pl.DeviceIdType.MESH
F32 = jnp.float32
BF16 = jnp.bfloat16
GROUPS = 4
OFF = 8


def each_level(start, stop, step, body, carry):
    def together(i, carry):
        for j in range(step):
            carry = body(start + i * step + j, carry)
        return carry

    return lax.fori_loop(0, (stop - start) // step, together, carry)


def lanes_of(shape):
    return lax.broadcasted_iota(jnp.int32, shape, len(shape) - 1)


def rows_of(shape):
    return lax.broadcasted_iota(jnp.int32, shape, len(shape) - 2)


def kernel(
    nx, ny, nz, m,
    t_hbm, uv_hbm, w_hbm, old_hbm, dz_hbm, r_hbm, wall_hbm,
    rhs, cur, head_pow, tail_pow, far_block,
    t, u_all, v_all, w, old, green, block_pow,
    theta, scale, inv_dz, up_coef, down_coef,
    pack, pack_got, edge, edge_got, edge_fix, side_fix, moment, moment_got, eights,
    dz_ref, r_ref,
    in_sem, halo_send, halo_recv, moment_send, moment_recv,
):
    gx = lax.axis_index("gx")
    gy = lax.axis_index("gy")
    east, west = lax.rem(gx + 1, nx), lax.rem(gx + nx - 1, nx)
    north, south = lax.rem(gy + 1, ny), lax.rem(gy + ny - 1, ny)
    q_rows = m // 4
    blocks = m // 8
    inside = pl.ds(OFF, m)

    loads = [
        pltpu.make_async_copy(r_hbm, r_ref, in_sem.at[0]),
        pltpu.make_async_copy(dz_hbm, dz_ref, in_sem.at[1]),
        pltpu.make_async_copy(t_hbm, t.at[pl.ds(1, nz), inside], in_sem.at[2]),
        pltpu.make_async_copy(uv_hbm.at[1], v_all, in_sem.at[3]),
        pltpu.make_async_copy(uv_hbm.at[0], u_all.at[:, inside], in_sem.at[4]),
        pltpu.make_async_copy(wall_hbm.at[0], t.at[0, inside], in_sem.at[5]),
        pltpu.make_async_copy(wall_hbm.at[1], t.at[nz + 1, inside], in_sem.at[6]),
        pltpu.make_async_copy(w_hbm, w.at[pl.ds(1, nz)], in_sem.at[7]),
        pltpu.make_async_copy(old_hbm, old, in_sem.at[8]),
    ]
    for load in loads[:4]:
        load.start()

    barrier = pltpu.get_barrier_semaphore()
    for s in range(1, nx):
        pl.semaphore_signal(
            barrier, inc=1, device_id={"gx": lax.rem(gx + s, nx)}, device_id_type=MESH
        )
    for j in (north, south):
        pl.semaphore_signal(barrier, inc=1, device_id={"gy": j}, device_id_type=MESH)

    for load in loads[4:]:
        load.start()

    loads[0].wait()
    loads[1].wait()
    for k in range(nz):
        scale[k:k + 1, :] = jnp.full((1, m), r_ref[k], F32)
        inv_dz[k:k + 1, :] = 1.0 / jnp.full((1, m), dz_ref[k], F32)
    down_coef[0:1, :] = inv_dz[0:1, :]
    up_coef[nz - 1:nz, :] = inv_dz[nz - 1:nz, :]
    for k in range(nz - 1):
        between = 2.0 / jnp.full((1, m), dz_ref[k] + dz_ref[k + 1], F32)
        up_coef[k:k + 1, :] = between
        down_coef[k + 1:k + 2, :] = between
    up_coef[...] = DIFF_Z * up_coef[...] * inv_dz[...]
    down_coef[...] = DIFF_Z * down_coef[...] * inv_dz[...]
    inv_dz[...] = (-0.25 * COURANT) * inv_dz[...]
    r = scale[...]
    s = 0.5 / jnp.sqrt(r)
    theta[...] = 2.0 * jnp.log1p(s + s * s / (1.0 + jnp.sqrt(1.0 + s * s)))
    scale[...] = 1.0 / jnp.sqrt(1.0 + 4.0 * r)
    th = theta[...]
    for b in range(blocks):
        block_pow[b] = jnp.exp((-8.0 * b) * th)

    def make_tables(k, carry):
        row = rows_of((8, m))
        lane = lanes_of((8, m))
        th = theta[pl.ds(k, 1), :]
        head_pow[k] = jnp.exp(-th * row.astype(F32))
        tail_pow[k] = jnp.exp(-th * (7 - row).astype(F32))
        return carry

    each_level(0, nz, 4, make_tables, 0)

    for load in loads[2:5]:
        load.wait()

    def make_pack(k, carry):
        pt, pv = carry
        pair = lanes_of((q_rows, m)) // 2
        for h in range(4):
            turn = 32 * h + 2 * k + 1
            mine = pair == 16 * h + k
            here = t[k + 1, OFF + h * q_rows:OFF + (h + 1) * q_rows, :]
            pt = jnp.where(mine, pltpu.roll(here, turn, 1), pt)
            pv = jnp.where(
                mine, pltpu.roll(v_all[k, h * q_rows:(h + 1) * q_rows, :], turn, 1), pv
            )
        edge[0, 0, pl.ds(k, 1), :] = t[k + 1, OFF + m - 1:OFF + m, :]
        edge[0, 1, pl.ds(k, 1), :] = u_all[k, OFF + m - 1:OFF + m, :]
        edge[1, 0, pl.ds(k, 1), :] = t[k + 1, OFF:OFF + 1, :]
        edge[1, 1, pl.ds(k, 1), :] = u_all[k, OFF:OFF + 1, :]
        return pt, pv

    blank = jnp.zeros((q_rows, m), F32)
    pt, pv = each_level(0, nz, 4, make_pack, (blank, blank))
    pack[0] = pt
    pack[1] = pv

    pl.semaphore_wait(barrier, nx + 1)

    def halo(src, dst, i, where):
        copy = pltpu.make_async_remote_copy(
            src_ref=src, dst_ref=dst, send_sem=halo_send.at[i], recv_sem=halo_recv.at[i],
            device_id=where, device_id_type=MESH,
        )
        copy.start()
        return copy

    halos = [
        halo(pack, pack_got.at[0], 0, {"gy": north}),
        halo(pack, pack_got.at[1], 1, {"gy": south}),
        halo(edge.at[0], edge_got.at[0], 2, {"gx": east}),
        halo(edge.at[1], edge_got.at[1], 3, {"gx": west}),
    ]

    for load in loads[5:]:
        load.wait()
    w[0] = -w[1]
    w[nz + 1] = -w[nz]

    def inner(k, carry):
        row = rows_of((q_rows, m))
        lane = lanes_of((q_rows, m))
        one = pl.ds(k, 1)
        up, down, idz = up_coef[one, :], down_coef[one, :], inv_dz[one, :]
        low_sum = jnp.zeros((8, m), F32)
        high_sum = jnp.zeros((8, m), F32)
        for h in range(4):
            rows = slice(h * q_rows, (h + 1) * q_rows)
            pad = slice(OFF + h * q_rows, OFF + (h + 1) * q_rows)
            after = slice(OFF + h * q_rows + 1, OFF + (h + 1) * q_rows + 1)
            before = slice(OFF + h * q_rows - 1, OFF + (h + 1) * q_rows - 1)
            here = t[k + 1, pad, :]
            u = u_all[k, pad, :]
            v = v_all[k, rows, :]
            fx = (u + u_all[k, after, :]) * (here + t[k + 1, after, :])
            gx_flux = (u_all[k, before, :] + u) * (t[k + 1, before, :] + here)
            if h == 3:
                fx = jnp.where(row == q_rows - 1, 0.0, fx)
            if h == 0:
                gx_flux = jnp.where(row == 0, 0.0, gx_flux)
            right = pltpu.roll(here, m - 1, 1)
            fy = (v + pltpu.roll(v, m - 1, 1)) * (here + right)
            fy = jnp.where(lane == m - 1, 0.0, fy)
            div = (fx - gx_flux) + (fy - pltpu.roll(fy, 1, 1))
            lap = jnp.where(lane == m - 1, 0.0, right) + jnp.where(
                lane == 0, 0.0, pltpu.roll(here, 1, 1)
            )
            below, above = t[k, pad, :], t[k + 2, pad, :]
            wk = w[k + 1, rows, :]
            fz = (wk + w[k + 2, rows, :]) * (here + above) - (w[k, rows, :] + wk) * (below + here)
            value = (
                (-0.25 * COURANT) * div
                + idz * fz
                + DIFF_Y * (lap - 2.0 * here)
                + (up * (above - here) - down * (here - below))
            )
            b = here + NEW_TERM_COEF * value + OLD_TERM_COEF * old[k, rows, :]
            cur[k, rows, :] = value
            rhs[k, rows, :] = b
            for i in range(4):
                c = 4 * h + i
                part = b[8 * i:8 * i + 8, :]
                low_sum = low_sum + block_pow[blocks - 1 - c, one, :] * part
                high_sum = high_sum + block_pow[c, one, :] * part
        eights[0, k] = tail_pow[k] * low_sum
        eights[1, k] = head_pow[k] * high_sum
        return carry

    each_level(0, nz, 4, inner, 0)

    lane1 = lanes_of((1, m))
    th_lane = jnp.zeros((1, m), F32)
    for k in range(nz):
        th_lane = jnp.where(lax.rem(lane1, 32) // 2 == k, theta[k:k + 1, :], th_lane)
    cell = rows_of((q_rows, m)) + (lanes_of((q_rows, m)) // 32) * q_rows
    weight_f = NEW_TERM_COEF * jnp.exp(-th_lane * cell.astype(F32))
    weight_g = NEW_TERM_COEF * jnp.exp(-th_lane * (m - 1 - cell).astype(F32))
    q_end = jnp.exp(-(m - 1.0) * th)
    sums_low = jnp.sum(eights[0], axis=1)
    sums_high = jnp.sum(eights[1], axis=1)

    for copy in halos:
        copy.wait_recv()

    first = lax.rem(lanes_of((q_rows, m)), 2) == 1
    near_t = jnp.where(
        first, pltpu.roll(pack_got[0, 0], 1, 1), pltpu.roll(pack_got[1, 0], m - 1, 1)
    )
    near_v = jnp.where(
        first, pltpu.roll(pack_got[0, 1], 1, 1), pltpu.roll(pack_got[1, 1], m - 1, 1)
    )
    flux = (pack[1] + near_v) * (pack[0] + near_t)
    fix = DIFF_Y * near_t + jnp.where(first, 0.25 * COURANT, -0.25 * COURANT) * flux
    side_fix[...] = fix
    low = (0.25 * COURANT) * (edge_got[0, 1] + edge[1, 1]) * (edge_got[0, 0] + edge[1, 0])
    top = (-0.25 * COURANT) * (edge_got[1, 1] + edge[0, 1]) * (edge_got[1, 0] + edge[0, 0])
    edge_fix[0] = low
    edge_fix[1] = top

    level = rows_of((nz, m))
    lane = lanes_of((nz, m))

    def spread(weights):
        line = jnp.sum(weights * fix, axis=0, keepdims=True)
        line = line + pltpu.roll(line, 32, 1)
        line = line + pltpu.roll(line, 64, 1)
        wide = jnp.broadcast_to(line, (nz, m))
        last = jnp.sum(jnp.where(lane == 2 * level, wide, 0.0), axis=1, keepdims=True)
        head = jnp.sum(jnp.where(lane == 2 * level + 1, wide, 0.0), axis=1, keepdims=True)
        return jnp.where(lane == 0, head, 0.0) + jnp.where(lane == m - 1, last, 0.0)

    moment[0] = sums_low + NEW_TERM_COEF * (q_end * low + top) + spread(weight_g)
    moment[1] = sums_high + NEW_TERM_COEF * (low + q_end * top) + spread(weight_f)

    sends = []
    upper = lax.div(gx, nx // 2)
    from_end = gx + upper * (nx - 1 - 2 * gx)
    for j in range(nx - 1):
        target = nx - 1 - j
        there = target - lax.div(from_end - target + nx, nx)
        there = there + upper * (nx - 1 - 2 * there)
        slot = lax.rem(there - gx + nx, nx) - 1
        copy = pltpu.make_async_remote_copy(
            src_ref=moment, dst_ref=moment_got.at[slot],
            send_sem=moment_send.at[j], recv_sem=moment_recv.at[slot],
            device_id={"gx": there}, device_id_type=MESH,
        )
        copy.start()
        sends.append(copy)

    def local_inverse(k, carry):
        row8 = rows_of((8, m))
        lane8 = lanes_of((8, m))
        th = theta[pl.ds(k, 1), :]
        level_scale = scale[pl.ds(k, 1), :]
        near = level_scale * jnp.exp(-th * jnp.abs(row8 - lane8).astype(F32))
        wrap = level_scale * jnp.exp(-th * (row8 - lane8 + m).astype(F32))
        for b0 in range(0, blocks, 2):
            full = jnp.concatenate(
                [
                    pltpu.roll(jnp.where(lane8 < m - 8 * c, near, wrap), 8 * c, 1)
                    if c
                    else near
                    for c in (b0, b0 + 1)
                ],
                axis=0,
            )
            high = full.astype(BF16)
            green[k, 8 * b0:8 * b0 + 16, 0:m] = high
            green[k, 8 * b0:8 * b0 + 16, m:2 * m] = (full - high.astype(F32)).astype(BF16)
        return carry

    each_level(0, nz, 4, local_inverse, 0)

    def local_solve(k, carry):
        lane = lanes_of((q_rows, m))
        row = rows_of((q_rows, m))
        side = (lane == 0) | (lane == m - 1)
        parts = []
        for h in range(4):
            rows = slice(h * q_rows, (h + 1) * q_rows)
            extra = jnp.where(
                side, pltpu.roll(side_fix[...], m - 1 - 32 * h - 2 * k, 1), 0.0
            )
            if h == 0:
                extra = extra + jnp.where(row == 0, edge_fix[0, pl.ds(k, 1), :], 0.0)
            if h == 3:
                extra = extra + jnp.where(row == q_rows - 1, edge_fix[1, pl.ds(k, 1), :], 0.0)
            cur[k, rows, :] = cur[k, rows, :] + extra
            parts.append(rhs[k, rows, :] + NEW_TERM_COEF * extra)
        b = jnp.concatenate(parts, axis=0)
        high = b.astype(BF16)
        pair = jnp.concatenate([high, (b - high.astype(F32)).astype(BF16)], axis=1)
        both = jnp.dot(
            green[k], jnp.concatenate([pair, pair], axis=0), preferred_element_type=F32
        )
        rhs[k] = both[:, 0:m] + both[:, m:2 * m]
        return carry

    each_level(0, nz, 4, local_solve, 0)

    step = jnp.exp(-float(m) * th)
    share = scale[...] * jnp.exp(-th) / (1.0 - jnp.exp(-float(m * nx) * th))
    powers = [jnp.ones_like(step)]
    for s in range(1, nx):
        powers.append(powers[-1] * step)
    from_low = powers[nx - 1] * moment[0]
    from_high = powers[nx - 1] * moment[1]

    for s in range(1, nx):
        pltpu.make_async_remote_copy(
            src_ref=moment, dst_ref=moment_got.at[s - 1],
            send_sem=moment_send.at[s - 1], recv_sem=moment_recv.at[s - 1],
            device_id={"gx": lax.rem(gx + s, nx)}, device_id_type=MESH,
        ).wait_recv()
    for s in range(1, nx):
        from_low = from_low + powers[s - 1] * moment_got[s - 1, 0]
        from_high = from_high + powers[nx - s - 1] * moment_got[s - 1, 1]
    from_low = share * from_low
    from_high = share * from_high
    for b in range(blocks):
        far_block[0, b] = block_pow[b] * from_low
        far_block[1, b] = block_pow[blocks - 1 - b] * from_high

    for copy in halos + sends:
        copy.wait_send()


def finish_kernel(nz, m, part_ref, cur_ref, head_pow, tail_pow, far_block, x_hbm, c_hbm, x, out_sem):
    blocks = m // 8
    stores = [pltpu.make_async_copy(cur_ref, c_hbm, out_sem.at[GROUPS])]
    stores[0].start()

    def finish(k, carry):
        head = head_pow[k]
        tail = tail_pow[k]
        for b in range(blocks):
            rows = slice(8 * b, 8 * b + 8)
            x[k, rows, :] = (
                part_ref[k, rows, :]
                + head * far_block[0, b, pl.ds(k, 1), :]
                + tail * far_block[1, b, pl.ds(k, 1), :]
            )
        return carry

    per = nz // GROUPS
    for part in range(GROUPS):
        each_level(part * per, (part + 1) * per, per, finish, 0)
        span = pl.ds(part * per, per)
        store = pltpu.make_async_copy(x.at[span], x_hbm.at[span], out_sem.at[part])
        store.start()
        stores.append(store)
    for store in stores:
        store.wait()


def on_device(
    initial_warmth_field,
    horizontal_motion_pair,
    z_directed_motion,
    earlier_rate_change,
    layer_depth_spacing,
    backward_spread_ratio,
    wall_warmth_bounds,
):
    nx = lax.axis_size("gx")
    ny = lax.axis_size("gy")
    nz, m, width = initial_warmth_field.shape
    assert nz == 16 and m == 128 and width == 128
    block = jax.ShapeDtypeStruct((nz, m, m), F32)
    anywhere = pl.BlockSpec(memory_space=pl.ANY)
    far_away = pl.BlockSpec(memory_space=pltpu.HBM)
    field = pltpu.VMEM((nz, m, m), F32)
    row = pltpu.VMEM((nz, m), F32)
    near = pl.BlockSpec(memory_space=pltpu.VMEM)
    carried = (
        field,
        field,
        pltpu.VMEM((nz, 8, m), F32),
        pltpu.VMEM((nz, 8, m), F32),
        pltpu.VMEM((2, m // 8, nz, m), F32),
    )
    between = pl.pallas_call(
        functools.partial(kernel, nx, ny, nz, m),
        out_shape=carried,
        in_specs=[far_away] * 7,
        out_specs=(near,) * 5,
        scratch_shapes=[
            pltpu.VMEM((nz + 2, m + 2 * OFF, m), F32),
            pltpu.VMEM((nz, m + 2 * OFF, m), F32),
            field,
            pltpu.VMEM((nz + 2, m, m), F32),
            field,
            pltpu.VMEM((nz, m, 2 * m), BF16),
            pltpu.VMEM((m // 8, nz, m), F32),
            row, row, row, row, row,
            pltpu.VMEM((2, m // 4, m), F32),
            pltpu.VMEM((2, 2, m // 4, m), F32),
            pltpu.VMEM((2, 2, nz, m), F32),
            pltpu.VMEM((2, 2, nz, m), F32),
            pltpu.VMEM((2, nz, m), F32),
            pltpu.VMEM((m // 4, m), F32),
            pltpu.VMEM((2, nz, m), F32),
            pltpu.VMEM((nx - 1, 2, nz, m), F32),
            pltpu.VMEM((2, nz, 8, m), F32),
            pltpu.SMEM((nz,), F32),
            pltpu.SMEM((nz,), F32),
            pltpu.SemaphoreType.DMA((9,)),
            pltpu.SemaphoreType.DMA((4,)),
            pltpu.SemaphoreType.DMA((4,)),
            pltpu.SemaphoreType.DMA((nx - 1,)),
            pltpu.SemaphoreType.DMA((nx - 1,)),
        ],
        compiler_params=pltpu.CompilerParams(
            collective_id=0, has_side_effects=True, vmem_limit_bytes=58 * 1024 * 1024
        ),
        cost_estimate=pl.CostEstimate(
            flops=16 * 2 * 128 * 256 * 256, bytes_accessed=8 * 1024 * 1024, transcendentals=0
        ),
    )(
        initial_warmth_field,
        horizontal_motion_pair,
        z_directed_motion,
        earlier_rate_change,
        layer_depth_spacing,
        backward_spread_ratio,
        wall_warmth_bounds,
    )
    return pl.pallas_call(
        functools.partial(finish_kernel, nz, m),
        out_shape=(block, block),
        in_specs=[near] * 5,
        out_specs=(anywhere, anywhere),
        scratch_shapes=[field, pltpu.SemaphoreType.DMA((GROUPS + 1,))],
        compiler_params=pltpu.CompilerParams(vmem_limit_bytes=16 * 1024 * 1024),
    )(*between)


def solution(mesh):
    in_specs = (
        P(None, "gx", "gy"),
        P(None, None, "gx", "gy"),
        P(None, "gx", "gy"),
        P(None, "gx", "gy"),
        P(),
        P(),
        P(None, "gx", "gy"),
    )
    out_specs = (P(None, "gx", "gy"), P(None, "gx", "gy"))
    return jax.shard_map(
        on_device, mesh=mesh, in_specs=in_specs, out_specs=out_specs, check_vma=False
    )
```

```python
import functools

import jax
import jax.numpy as jnp
from jax import lax
from jax.experimental import pallas as pl
from jax.experimental.pallas import tpu as pltpu
from jax.sharding import PartitionSpec as P

COURANT = 0.5
DIFF_Y = 0.2
DIFF_Z = 0.25
NEW_TERM_COEF = 0.75
OLD_TERM_COEF = -5.0 / 12.0

MESH = pl.DeviceIdType.MESH
F32 = jnp.float32
BF16 = jnp.bfloat16
GROUPS = 4
OFF = 8


def each_level(start, stop, step, body, carry):
    def together(i, carry):
        for j in range(step):
            carry = body(start + i * step + j, carry)
        return carry

    return lax.fori_loop(0, (stop - start) // step, together, carry)


def lanes_of(shape):
    return lax.broadcasted_iota(jnp.int32, shape, len(shape) - 1)


def rows_of(shape):
    return lax.broadcasted_iota(jnp.int32, shape, len(shape) - 2)


def kernel(
    nx, ny, nz, m,
    t_hbm, uv_hbm, w_hbm, old_hbm, dz_hbm, r_hbm, wall_hbm,
    rhs, cur, head_pow, tail_pow, far_block,
    t, u_all, v_all, w, old, green, block_pow,
    theta, scale, inv_dz, up_coef, down_coef,
    pack, pack_got, edge, edge_got, edge_fix, side_fix, moment, moment_got, eights,
    dz_ref, r_ref,
    in_sem, halo_send, halo_recv, moment_send, moment_recv,
):
    gx = lax.axis_index("gx")
    gy = lax.axis_index("gy")
    east, west = lax.rem(gx + 1, nx), lax.rem(gx + nx - 1, nx)
    north, south = lax.rem(gy + 1, ny), lax.rem(gy + ny - 1, ny)
    q_rows = m // 4
    blocks = m // 8
    inside = pl.ds(OFF, m)

    loads = [
        pltpu.make_async_copy(r_hbm, r_ref, in_sem.at[0]),
        pltpu.make_async_copy(dz_hbm, dz_ref, in_sem.at[1]),
        pltpu.make_async_copy(t_hbm, t.at[pl.ds(1, nz), inside], in_sem.at[2]),
        pltpu.make_async_copy(uv_hbm.at[1], v_all, in_sem.at[3]),
        pltpu.make_async_copy(uv_hbm.at[0], u_all.at[:, inside], in_sem.at[4]),
        pltpu.make_async_copy(wall_hbm.at[0], t.at[0, inside], in_sem.at[5]),
        pltpu.make_async_copy(wall_hbm.at[1], t.at[nz + 1, inside], in_sem.at[6]),
        pltpu.make_async_copy(w_hbm, w.at[pl.ds(1, nz)], in_sem.at[7]),
        pltpu.make_async_copy(old_hbm, old, in_sem.at[8]),
    ]
    for load in loads[:4]:
        load.start()

    barrier = pltpu.get_barrier_semaphore()
    for s in range(1, nx):
        pl.semaphore_signal(
            barrier, inc=1, device_id={"gx": lax.rem(gx + s, nx)}, device_id_type=MESH
        )
    for j in (north, south):
        pl.semaphore_signal(barrier, inc=1, device_id={"gy": j}, device_id_type=MESH)

    for load in loads[4:]:
        load.start()

    loads[0].wait()
    loads[1].wait()
    for k in range(nz):
        scale[k:k + 1, :] = jnp.full((1, m), r_ref[k], F32)
        inv_dz[k:k + 1, :] = 1.0 / jnp.full((1, m), dz_ref[k], F32)
    down_coef[0:1, :] = inv_dz[0:1, :]
    up_coef[nz - 1:nz, :] = inv_dz[nz - 1:nz, :]
    for k in range(nz - 1):
        between = 2.0 / jnp.full((1, m), dz_ref[k] + dz_ref[k + 1], F32)
        up_coef[k:k + 1, :] = between
        down_coef[k + 1:k + 2, :] = between
    up_coef[...] = DIFF_Z * up_coef[...] * inv_dz[...]
    down_coef[...] = DIFF_Z * down_coef[...] * inv_dz[...]
    inv_dz[...] = (-0.25 * COURANT) * inv_dz[...]
    r = scale[...]
    s = 0.5 / jnp.sqrt(r)
    theta[...] = 2.0 * jnp.log1p(s + s * s / (1.0 + jnp.sqrt(1.0 + s * s)))
    scale[...] = 1.0 / jnp.sqrt(1.0 + 4.0 * r)
    th = theta[...]
    for b in range(blocks):
        block_pow[b] = jnp.exp((-8.0 * b) * th)

    def make_tables(k, carry):
        row = rows_of((8, m))
        lane = lanes_of((8, m))
        th = theta[pl.ds(k, 1), :]
        head_pow[k] = jnp.exp(-th * row.astype(F32))
        tail_pow[k] = jnp.exp(-th * (7 - row).astype(F32))
        return carry

    each_level(0, nz, 4, make_tables, 0)

    for load in loads[2:5]:
        load.wait()

    def make_pack(k, carry):
        pt, pv = carry
        pair = lanes_of((q_rows, m)) // 2
        for h in range(4):
            turn = 32 * h + 2 * k + 1
            mine = pair == 16 * h + k
            here = t[k + 1, OFF + h * q_rows:OFF + (h + 1) * q_rows, :]
            pt = jnp.where(mine, pltpu.roll(here, turn, 1), pt)
            pv = jnp.where(
                mine, pltpu.roll(v_all[k, h * q_rows:(h + 1) * q_rows, :], turn, 1), pv
            )
        edge[0, 0, pl.ds(k, 1), :] = t[k + 1, OFF + m - 1:OFF + m, :]
        edge[0, 1, pl.ds(k, 1), :] = u_all[k, OFF + m - 1:OFF + m, :]
        edge[1, 0, pl.ds(k, 1), :] = t[k + 1, OFF:OFF + 1, :]
        edge[1, 1, pl.ds(k, 1), :] = u_all[k, OFF:OFF + 1, :]
        return pt, pv

    blank = jnp.zeros((q_rows, m), F32)
    pt, pv = each_level(0, nz, 4, make_pack, (blank, blank))
    pack[0] = pt
    pack[1] = pv

    pl.semaphore_wait(barrier, nx + 1)

    def halo(src, dst, i, where):
        copy = pltpu.make_async_remote_copy(
            src_ref=src, dst_ref=dst, send_sem=halo_send.at[i], recv_sem=halo_recv.at[i],
            device_id=where, device_id_type=MESH,
        )
        copy.start()
        return copy

    halos = [
        halo(pack, pack_got.at[0], 0, {"gy": north}),
        halo(pack, pack_got.at[1], 1, {"gy": south}),
        halo(edge.at[0], edge_got.at[0], 2, {"gx": east}),
        halo(edge.at[1], edge_got.at[1], 3, {"gx": west}),
    ]

    for load in loads[5:]:
        load.wait()
    w[0] = -w[1]
    w[nz + 1] = -w[nz]

    def inner(k, carry):
        row = rows_of((q_rows, m))
        lane = lanes_of((q_rows, m))
        one = pl.ds(k, 1)
        up, down, idz = up_coef[one, :], down_coef[one, :], inv_dz[one, :]
        low_sum = jnp.zeros((8, m), F32)
        high_sum = jnp.zeros((8, m), F32)
        for h in range(4):
            rows = slice(h * q_rows, (h + 1) * q_rows)
            pad = slice(OFF + h * q_rows, OFF + (h + 1) * q_rows)
            after = slice(OFF + h * q_rows + 1, OFF + (h + 1) * q_rows + 1)
            before = slice(OFF + h * q_rows - 1, OFF + (h + 1) * q_rows - 1)
            here = t[k + 1, pad, :]
            u = u_all[k, pad, :]
            v = v_all[k, rows, :]
            fx = (u + u_all[k, after, :]) * (here + t[k + 1, after, :])
            gx_flux = (u_all[k, before, :] + u) * (t[k + 1, before, :] + here)
            if h == 3:
                fx = jnp.where(row == q_rows - 1, 0.0, fx)
            if h == 0:
                gx_flux = jnp.where(row == 0, 0.0, gx_flux)
            right = pltpu.roll(here, m - 1, 1)
            fy = (v + pltpu.roll(v, m - 1, 1)) * (here + right)
            fy = jnp.where(lane == m - 1, 0.0, fy)
            div = (fx - gx_flux) + (fy - pltpu.roll(fy, 1, 1))
            lap = jnp.where(lane == m - 1, 0.0, right) + jnp.where(
                lane == 0, 0.0, pltpu.roll(here, 1, 1)
            )
            below, above = t[k, pad, :], t[k + 2, pad, :]
            wk = w[k + 1, rows, :]
            fz = (wk + w[k + 2, rows, :]) * (here + above) - (w[k, rows, :] + wk) * (below + here)
            value = (
                (-0.25 * COURANT) * div
                + idz * fz
                + DIFF_Y * (lap - 2.0 * here)
                + (up * (above - here) - down * (here - below))
            )
            b = here + NEW_TERM_COEF * value + OLD_TERM_COEF * old[k, rows, :]
            cur[k, rows, :] = value
            rhs[k, rows, :] = b
            for i in range(4):
                c = 4 * h + i
                part = b[8 * i:8 * i + 8, :]
                low_sum = low_sum + block_pow[blocks - 1 - c, one, :] * part
                high_sum = high_sum + block_pow[c, one, :] * part
        eights[0, k] = tail_pow[k] * low_sum
        eights[1, k] = head_pow[k] * high_sum
        return carry

    each_level(0, nz, 2, inner, 0)

    lane1 = lanes_of((1, m))
    th_lane = jnp.zeros((1, m), F32)
    for k in range(nz):
        th_lane = jnp.where(lax.rem(lane1, 32) // 2 == k, theta[k:k + 1, :], th_lane)
    cell = rows_of((q_rows, m)) + (lanes_of((q_rows, m)) // 32) * q_rows
    weight_f = NEW_TERM_COEF * jnp.exp(-th_lane * cell.astype(F32))
    weight_g = NEW_TERM_COEF * jnp.exp(-th_lane * (m - 1 - cell).astype(F32))
    q_end = jnp.exp(-(m - 1.0) * th)
    sums_low = jnp.sum(eights[0], axis=1)
    sums_high = jnp.sum(eights[1], axis=1)

    for copy in halos:
        copy.wait_recv()

    first = lax.rem(lanes_of((q_rows, m)), 2) == 1
    near_t = jnp.where(
        first, pltpu.roll(pack_got[0, 0], 1, 1), pltpu.roll(pack_got[1, 0], m - 1, 1)
    )
    near_v = jnp.where(
        first, pltpu.roll(pack_got[0, 1], 1, 1), pltpu.roll(pack_got[1, 1], m - 1, 1)
    )
    flux = (pack[1] + near_v) * (pack[0] + near_t)
    fix = DIFF_Y * near_t + jnp.where(first, 0.25 * COURANT, -0.25 * COURANT) * flux
    side_fix[...] = fix
    low = (0.25 * COURANT) * (edge_got[0, 1] + edge[1, 1]) * (edge_got[0, 0] + edge[1, 0])
    top = (-0.25 * COURANT) * (edge_got[1, 1] + edge[0, 1]) * (edge_got[1, 0] + edge[0, 0])
    edge_fix[0] = low
    edge_fix[1] = top

    level = rows_of((nz, m))
    lane = lanes_of((nz, m))

    def spread(weights):
        line = jnp.sum(weights * fix, axis=0, keepdims=True)
        line = line + pltpu.roll(line, 32, 1)
        line = line + pltpu.roll(line, 64, 1)
        wide = jnp.broadcast_to(line, (nz, m))
        last = jnp.sum(jnp.where(lane == 2 * level, wide, 0.0), axis=1, keepdims=True)
        head = jnp.sum(jnp.where(lane == 2 * level + 1, wide, 0.0), axis=1, keepdims=True)
        return jnp.where(lane == 0, head, 0.0) + jnp.where(lane == m - 1, last, 0.0)

    moment[0] = sums_low + NEW_TERM_COEF * (q_end * low + top) + spread(weight_g)
    moment[1] = sums_high + NEW_TERM_COEF * (low + q_end * top) + spread(weight_f)

    sends = []
    upper = lax.div(gx, nx // 2)
    from_end = gx + upper * (nx - 1 - 2 * gx)
    for j in range(nx - 1):
        target = nx - 1 - j
        there = target - lax.div(from_end - target + nx, nx)
        there = there + upper * (nx - 1 - 2 * there)
        slot = lax.rem(there - gx + nx, nx) - 1
        copy = pltpu.make_async_remote_copy(
            src_ref=moment, dst_ref=moment_got.at[slot],
            send_sem=moment_send.at[j], recv_sem=moment_recv.at[slot],
            device_id={"gx": there}, device_id_type=MESH,
        )
        copy.start()
        sends.append(copy)

    def local_inverse(k, carry):
        row8 = rows_of((8, m))
        lane8 = lanes_of((8, m))
        th = theta[pl.ds(k, 1), :]
        level_scale = scale[pl.ds(k, 1), :]
        near = level_scale * jnp.exp(-th * jnp.abs(row8 - lane8).astype(F32))
        wrap = level_scale * jnp.exp(-th * (row8 - lane8 + m).astype(F32))
        for b0 in range(0, blocks, 2):
            full = jnp.concatenate(
                [
                    pltpu.roll(jnp.where(lane8 < m - 8 * c, near, wrap), 8 * c, 1)
                    if c
                    else near
                    for c in (b0, b0 + 1)
                ],
                axis=0,
            )
            high = full.astype(BF16)
            green[k, 8 * b0:8 * b0 + 16, 0:m] = high
            green[k, 8 * b0:8 * b0 + 16, m:2 * m] = (full - high.astype(F32)).astype(BF16)
        return carry

    each_level(0, nz, 4, local_inverse, 0)

    def local_solve(k, carry):
        lane = lanes_of((q_rows, m))
        row = rows_of((q_rows, m))
        side = (lane == 0) | (lane == m - 1)
        parts = []
        for h in range(4):
            rows = slice(h * q_rows, (h + 1) * q_rows)
            extra = jnp.where(
                side, pltpu.roll(side_fix[...], m - 1 - 32 * h - 2 * k, 1), 0.0
            )
            if h == 0:
                extra = extra + jnp.where(row == 0, edge_fix[0, pl.ds(k, 1), :], 0.0)
            if h == 3:
                extra = extra + jnp.where(row == q_rows - 1, edge_fix[1, pl.ds(k, 1), :], 0.0)
            cur[k, rows, :] = cur[k, rows, :] + extra
            parts.append(rhs[k, rows, :] + NEW_TERM_COEF * extra)
        b = jnp.concatenate(parts, axis=0)
        high = b.astype(BF16)
        pair = jnp.concatenate([high, (b - high.astype(F32)).astype(BF16)], axis=1)
        both = jnp.dot(
            green[k], jnp.concatenate([pair, pair], axis=0), preferred_element_type=F32
        )
        rhs[k] = both[:, 0:m] + both[:, m:2 * m]
        return carry

    each_level(0, nz, 4, local_solve, 0)

    step = jnp.exp(-float(m) * th)
    share = scale[...] * jnp.exp(-th) / (1.0 - jnp.exp(-float(m * nx) * th))
    powers = [jnp.ones_like(step)]
    for s in range(1, nx):
        powers.append(powers[-1] * step)
    from_low = powers[nx - 1] * moment[0]
    from_high = powers[nx - 1] * moment[1]

    for s in range(1, nx):
        pltpu.make_async_remote_copy(
            src_ref=moment, dst_ref=moment_got.at[s - 1],
            send_sem=moment_send.at[s - 1], recv_sem=moment_recv.at[s - 1],
            device_id={"gx": lax.rem(gx + s, nx)}, device_id_type=MESH,
        ).wait_recv()
    for s in range(1, nx):
        from_low = from_low + powers[s - 1] * moment_got[s - 1, 0]
        from_high = from_high + powers[nx - s - 1] * moment_got[s - 1, 1]
    from_low = share * from_low
    from_high = share * from_high
    for b in range(blocks):
        far_block[0, b] = block_pow[b] * from_low
        far_block[1, b] = block_pow[blocks - 1 - b] * from_high

    for copy in halos + sends:
        copy.wait_send()


def finish_kernel(nz, m, part_ref, cur_ref, head_pow, tail_pow, far_block, x_hbm, c_hbm, x, out_sem):
    blocks = m // 8
    stores = [pltpu.make_async_copy(cur_ref, c_hbm, out_sem.at[GROUPS])]
    stores[0].start()

    def finish(k, carry):
        head = head_pow[k]
        tail = tail_pow[k]
        for b in range(blocks):
            rows = slice(8 * b, 8 * b + 8)
            x[k, rows, :] = (
                part_ref[k, rows, :]
                + head * far_block[0, b, pl.ds(k, 1), :]
                + tail * far_block[1, b, pl.ds(k, 1), :]
            )
        return carry

    per = nz // GROUPS
    for part in range(GROUPS):
        each_level(part * per, (part + 1) * per, per, finish, 0)
        span = pl.ds(part * per, per)
        store = pltpu.make_async_copy(x.at[span], x_hbm.at[span], out_sem.at[part])
        store.start()
        stores.append(store)
    for store in stores:
        store.wait()


def on_device(
    initial_warmth_field,
    horizontal_motion_pair,
    z_directed_motion,
    earlier_rate_change,
    layer_depth_spacing,
    backward_spread_ratio,
    wall_warmth_bounds,
):
    nx = lax.axis_size("gx")
    ny = lax.axis_size("gy")
    nz, m, width = initial_warmth_field.shape
    assert nz == 16 and m == 128 and width == 128
    block = jax.ShapeDtypeStruct((nz, m, m), F32)
    anywhere = pl.BlockSpec(memory_space=pl.ANY)
    far_away = pl.BlockSpec(memory_space=pltpu.HBM)
    field = pltpu.VMEM((nz, m, m), F32)
    row = pltpu.VMEM((nz, m), F32)
    near = pl.BlockSpec(memory_space=pltpu.VMEM)
    carried = (
        field,
        field,
        pltpu.VMEM((nz, 8, m), F32),
        pltpu.VMEM((nz, 8, m), F32),
        pltpu.VMEM((2, m // 8, nz, m), F32),
    )
    between = pl.pallas_call(
        functools.partial(kernel, nx, ny, nz, m),
        out_shape=carried,
        in_specs=[far_away] * 7,
        out_specs=(near,) * 5,
        scratch_shapes=[
            pltpu.VMEM((nz + 2, m + 2 * OFF, m), F32),
            pltpu.VMEM((nz, m + 2 * OFF, m), F32),
            field,
            pltpu.VMEM((nz + 2, m, m), F32),
            field,
            pltpu.VMEM((nz, m, 2 * m), BF16),
            pltpu.VMEM((m // 8, nz, m), F32),
            row, row, row, row, row,
            pltpu.VMEM((2, m // 4, m), F32),
            pltpu.VMEM((2, 2, m // 4, m), F32),
            pltpu.VMEM((2, 2, nz, m), F32),
            pltpu.VMEM((2, 2, nz, m), F32),
            pltpu.VMEM((2, nz, m), F32),
            pltpu.VMEM((m // 4, m), F32),
            pltpu.VMEM((2, nz, m), F32),
            pltpu.VMEM((nx - 1, 2, nz, m), F32),
            pltpu.VMEM((2, nz, 8, m), F32),
            pltpu.SMEM((nz,), F32),
            pltpu.SMEM((nz,), F32),
            pltpu.SemaphoreType.DMA((9,)),
            pltpu.SemaphoreType.DMA((4,)),
            pltpu.SemaphoreType.DMA((4,)),
            pltpu.SemaphoreType.DMA((nx - 1,)),
            pltpu.SemaphoreType.DMA((nx - 1,)),
        ],
        compiler_params=pltpu.CompilerParams(
            collective_id=0, has_side_effects=True, vmem_limit_bytes=58 * 1024 * 1024
        ),
        cost_estimate=pl.CostEstimate(
            flops=16 * 2 * 128 * 256 * 256, bytes_accessed=8 * 1024 * 1024, transcendentals=0
        ),
    )(
        initial_warmth_field,
        horizontal_motion_pair,
        z_directed_motion,
        earlier_rate_change,
        layer_depth_spacing,
        backward_spread_ratio,
        wall_warmth_bounds,
    )
    return pl.pallas_call(
        functools.partial(finish_kernel, nz, m),
        out_shape=(block, block),
        in_specs=[near] * 5,
        out_specs=(anywhere, anywhere),
        scratch_shapes=[field, pltpu.SemaphoreType.DMA((GROUPS + 1,))],
        compiler_params=pltpu.CompilerParams(vmem_limit_bytes=16 * 1024 * 1024),
    )(*between)


def solution(mesh):
    in_specs = (
        P(None, "gx", "gy"),
        P(None, None, "gx", "gy"),
        P(None, "gx", "gy"),
        P(None, "gx", "gy"),
        P(),
        P(),
        P(None, "gx", "gy"),
    )
    out_specs = (P(None, "gx", "gy"), P(None, "gx", "gy"))
    return jax.shard_map(
        on_device, mesh=mesh, in_specs=in_specs, out_specs=out_specs, check_vma=False
    )
```
